32 devices in a mesh: dp: 16 (over z, y, x), tensor: 2 (over core).
Axes of the slice: x: 2, y: 2, z: 4, core: 2. Of those that a mesh axis runs over, the one named last changes fastest.
Arguments:
- tokens: bfloat16 [32768, 1280], P(('dp', 'tensor')), may hold values from -6 to 6
- cotangent: bfloat16 [32768, 1280], P(('dp', 'tensor')), may hold values from -6 to 6
- picture_ids: int32 [32768], P('dp'), may hold values from 0 to 3, as said below
- positions: int32 [2, 32768], P(None, 'dp'), may hold values from 0 to 383, as said below
- valid: int32 [32768], P('dp'), may hold values from 0 to 1, as said below
- norm1_gain: bfloat16 [1280], replicated, may hold values from 0.099609375 to 1.8984375
- norm1_bias: bfloat16 [1280], replicated, may hold values from -3 to 3
- qkv_weight: bfloat16 [1280, 3, 1280], P('dp', None, 'tensor'), may hold values from -0.15625 to 0.15625
- qkv_bias: bfloat16 [3, 1280], replicated, may hold values from -3 to 3
- proj_weight: bfloat16 [1280, 1280], P('tensor', 'dp'), may hold values from -1 to 1
- proj_bias: bfloat16 [1280], replicated, may hold values from -3 to 3
- norm2_gain: bfloat16 [1280], replicated, may hold values from 0.099609375 to 1.8984375
- norm2_bias: bfloat16 [1280], replicated, may hold values from -3 to 3
- fc1_weight: bfloat16 [1280, 5120], P('dp', 'tensor'), may hold values from -0.15625 to 0.15625
- fc1_bias: bfloat16 [5120], replicated, may hold values from -3 to 3
- fc2_weight: bfloat16 [5120, 1280], P('tensor', 'dp'), may hold values from -0.078125 to 0.078125
- fc2_bias: bfloat16 [1280], replicated, may hold values from -3 to 3
Outputs:
- output: float32 [32768, 1280], P(('dp', 'tensor'))
- input_grad: float32 [32768, 1280], P(('dp', 'tensor'))
- norm1_gain_grad: float32 [1280], replicated
- norm1_bias_grad: float32 [1280], replicated
- qkv_weight_grad: float32 [1280, 3, 1280], P('dp', None, 'tensor')
- qkv_bias_grad: float32 [3, 1280], replicated
- proj_weight_grad: float32 [1280, 1280], P('tensor', 'dp')
- proj_bias_grad: float32 [1280], replicated
- norm2_gain_grad: float32 [1280], replicated
- norm2_bias_grad: float32 [1280], replicated
- fc1_weight_grad: float32 [1280, 5120], P('dp', 'tensor')
- fc1_bias_grad: float32 [5120], replicated
- fc2_weight_grad: float32 [5120, 1280], P('tensor', 'dp')
- fc2_bias_grad: float32 [1280], replicated
The draws below stay inside these ranges and needn't reach their ends.
Inputs may be any that keep to these rules, and one draw needn't show every extreme that they name: `picture_ids`: each row of 2048 patches holds four pictures in order, ids 0 to 3 never falling; the first picture has 1024 to 1536 patches, every picture at least one valid patch; padding patches come at a row's end and carry id 3. A picture's patches run row by row over a grid of 4 to 32 columns; padding patches have positions 0. In each row the valid patches come first; up to 256 padding patches follow, exactly 256 in the first row.
All inputs are finite; a program needn't handle non-finite values.
Results may differ from the reference program's by a relative error of at most 0.023.
Values may be sent and summed in bfloat16 or wider, within the bound.
No kernel may reach another device: no remote copies, remote signals or barrier semaphores. Data moves between devices by JAX's collectives and lax.ppermute only.
A program may use at most 384 MiB of HBM per device.

```python
import jax
import jax.numpy as jnp
from jax import lax

D = 1280
HEADS = 16
HEAD_DIM = 80
FF = 5120
ROW_LEN = 2048
TOKENS = 32768


def layout(key):
    base = jax.random.fold_in(key, 17)
    parts = jax.random.split(base, 5)
    count = TOKENS // ROW_LEN
    padding = jax.random.randint(parts[0], (count,), 0, ROW_LEN // 8 + 1)
    padding = padding.at[0].set(ROW_LEN // 8)
    used = ROW_LEN - padding
    first = jax.random.randint(parts[1], (count,), ROW_LEN // 2, 3 * ROW_LEN // 4 + 1)
    first = first.at[0].set(3 * ROW_LEN // 4)
    remain = used - first
    cut_one = jax.random.randint(parts[2], (count,), 1, remain - 1)
    cut_two = jax.random.randint(parts[3], (count,), cut_one + 1, remain)
    starts = jnp.stack([jnp.zeros_like(first), first, first + cut_one, first + cut_two], axis=1)
    widths = jax.random.randint(parts[4], (count, 4), 4, min(33, ROW_LEN // 16 + 1))
    widths = widths.at[0, 0].set(4)
    place = jnp.arange(ROW_LEN, dtype=jnp.int32)[None, :]
    picture = (place >= starts[:, 1:2]).astype(jnp.int32) + (place >= starts[:, 2:3]).astype(jnp.int32) + (place >= starts[:, 3:4]).astype(jnp.int32)
    begin = jnp.take_along_axis(starts, picture, axis=1)
    across = jnp.take_along_axis(widths, picture, axis=1)
    offset = place - begin
    live = (place < used[:, None]).astype(jnp.int32)
    grid_rows = jnp.where(live > 0, offset // across, 0)
    grid_cols = jnp.where(live > 0, offset % across, 0)
    return (picture.reshape(-1), jnp.stack([grid_rows.reshape(-1), grid_cols.reshape(-1)]), live.reshape(-1))


def draw_picture_ids(key, part):
    return layout(key)[0]


def draw_positions(key, part):
    return layout(key)[1]


def draw_valid(key, part):
    return layout(key)[2]


def level_of(own_key, extent, pieces, low, high):
    level, own = 1.0, jax.random.fold_in(own_key, 6)
    for position, shards_of in pieces:
        heights = jnp.exp(jax.random.uniform(jax.random.fold_in(own, position), (shards_of,), jnp.float32, low / len(pieces), high / len(pieces)))
        level = level * jnp.repeat(heights, extent[position] // shards_of).reshape([-1 if axis == position else 1 for axis in range(len(extent))])
    return level


def centred(own_key, dims, deviation, reach, pieces=(), kind=jnp.bfloat16):
    values = deviation * jax.random.normal(own_key, dims, jnp.float32)
    if pieces:
        values = values * level_of(own_key, dims, pieces, -0.22, 0.18)
    return jnp.clip(values, -reach, reach).astype(kind)


def setup_inputs(seed: int = 0) -> dict:
    seeds = jax.random.split(jax.random.key(seed), 18)
    tokens = centred(seeds[0], (TOKENS, D), 1.0, 6.0, ((0, 32),))
    cotangent = centred(seeds[1], (TOKENS, D), 1.0, 6.0, ((0, 32),))
    picture_ids = draw_picture_ids(jax.random.fold_in(seeds[17], 71), 0)
    positions = draw_positions(jax.random.fold_in(seeds[17], 71), 0)
    valid = draw_valid(jax.random.fold_in(seeds[17], 71), 0)
    norm1_gain = jnp.clip(1.0 + 0.18 * jax.random.normal(seeds[5], (D,), jnp.float32), 0.099609375, 1.8984375).astype(jnp.bfloat16)
    norm1_bias = centred(seeds[6], (D,), 0.5, 3.0)
    qkv_weight = centred(seeds[7], (D, 3, D), D ** -0.5, 0.15625, ((0, 16), (2, 2)))
    qkv_bias = centred(seeds[8], (3, D), 0.5, 3.0)
    proj_weight = centred(seeds[9], (D, D), (D // 32) ** -0.5, 1.0, ((0, 2), (1, 16)))
    proj_bias = centred(seeds[10], (D,), 0.5, 3.0)
    norm2_gain = jnp.clip(1.0 + 0.18 * jax.random.normal(seeds[11], (D,), jnp.float32), 0.099609375, 1.8984375).astype(jnp.bfloat16)
    norm2_bias = centred(seeds[12], (D,), 0.5, 3.0)
    fc1_weight = centred(seeds[13], (D, FF), D ** -0.5, 0.15625, ((0, 16), (1, 2)))
    fc1_bias = centred(seeds[14], (FF,), 0.5, 3.0)
    fc2_weight = centred(seeds[15], (FF, D), FF ** -0.5, 0.078125, ((0, 2), (1, 16)))
    fc2_bias = centred(seeds[16], (D,), 0.5, 3.0)
    return dict(tokens=tokens, cotangent=cotangent, picture_ids=picture_ids, positions=positions, valid=valid, norm1_gain=norm1_gain, norm1_bias=norm1_bias, qkv_weight=qkv_weight, qkv_bias=qkv_bias, proj_weight=proj_weight, proj_bias=proj_bias, norm2_gain=norm2_gain, norm2_bias=norm2_bias, fc1_weight=fc1_weight, fc1_bias=fc1_bias, fc2_weight=fc2_weight, fc2_bias=fc2_bias)


EPS = 1e-06
HIGH = lax.Precision.HIGHEST

@jax.custom_vjp
def low(v):
    return lax.optimization_barrier(v.astype(jnp.bfloat16)).astype(jnp.float32)

@jax.custom_vjp
def low_back(v):
    return v

def low_keep(v):
    return (low(v), None)

def low_pass(kept, grad):
    return (grad,)

def back_keep(v):
    return (v, None)

def back_low(kept, grad):
    return (low(grad),)
low.defvjp(low_keep, low_pass)
low_back.defvjp(back_keep, back_low)

def matmul(left, right):
    return jnp.dot(left, right, precision=HIGH, preferred_element_type=jnp.float32)

def layer_norm(values, gain, shift):
    center = values - lax.optimization_barrier(jnp.mean(values, axis=-1, keepdims=True))
    spread = lax.optimization_barrier(jnp.mean(center * center, axis=-1, keepdims=True))
    return center * lax.rsqrt(spread + EPS) * gain + shift

def rope_tables(place):
    quarter = HEAD_DIM // 4
    freqs = 10000.0 ** (-2.0 * jnp.arange(quarter, dtype=jnp.float32) / (HEAD_DIM // 2))
    along_rows = place[0].astype(jnp.float32)[:, None] * freqs[None, :]
    along_cols = place[1].astype(jnp.float32)[:, None] * freqs[None, :]
    theta = jnp.concatenate([along_rows, along_cols, along_rows, along_cols], axis=1)
    return (jnp.cos(theta)[:, None, :], jnp.sin(theta)[:, None, :])

def rotate(values, cosine, sine):
    half = values.shape[-1] // 2
    turned = jnp.concatenate([-values[..., half:], values[..., :half]], axis=-1)
    return values * cosine + turned * sine

def attention(queries, keys, values, picture, live):
    length = queries.shape[0]
    block = min(512, length)
    count = length // block
    scale = HEAD_DIM ** (-0.5)

    def one_block(packed):
        query_block, id_block = packed
        scores = low_back(jnp.einsum('qhd,khd->hqk', query_block, keys, precision=HIGH) * scale)
        allowed = (id_block[:, None] == picture[None, :]) & (live[None, :] > 0)
        scores = jnp.where(allowed[None], scores, -1e+30)
        peak = lax.optimization_barrier(jnp.max(scores, axis=-1, keepdims=True))
        shifted = jnp.exp(scores - peak)
        probs = low(shifted / lax.optimization_barrier(jnp.sum(shifted, axis=-1, keepdims=True)))
        return jnp.einsum('hqk,khd->qhd', probs, values, precision=HIGH)
    blocks = lax.map(jax.checkpoint(one_block), (queries.reshape(count, block, HEADS, HEAD_DIM), picture.reshape(count, block)))
    return blocks.reshape(length, HEADS, HEAD_DIM)

def row_forward(inputs, picture, place, live, norm1_gain, norm1_bias, qkv_weight, qkv_bias, proj_weight, proj_bias, norm2_gain, norm2_bias, fc1_weight, fc1_bias, fc2_weight, fc2_bias):
    length = inputs.shape[0]
    normed = low(layer_norm(inputs, norm1_gain, norm1_bias))
    qkv = low_back(matmul(normed, qkv_weight.reshape(D, 3 * D)) + qkv_bias.reshape(3 * D))
    split = qkv.reshape(length, 3, HEADS, HEAD_DIM)
    cosine, sine = rope_tables(place)
    queries = low(rotate(split[:, 0], cosine, sine))
    keys = low(rotate(split[:, 1], cosine, sine))
    values = low(split[:, 2])
    mixed = attention(queries, keys, values, picture, live)
    mixed = low_back(low(mixed)).reshape(length, D)
    attn = low_back(matmul(mixed, proj_weight) + proj_bias)
    middle = inputs + attn
    normed_two = low(layer_norm(middle, norm2_gain, norm2_bias))
    hidden_pre = low_back(matmul(normed_two, fc1_weight) + fc1_bias)
    hidden = low(hidden_pre * jax.nn.sigmoid(1.702 * hidden_pre))
    branch = low_back(matmul(hidden, fc2_weight) + fc2_bias)
    return middle + branch

def reference(tokens, cotangent, picture_ids, positions, valid, norm1_gain, norm1_bias, qkv_weight, qkv_bias, proj_weight, proj_bias, norm2_gain, norm2_bias, fc1_weight, fc1_bias, fc2_weight, fc2_bias):
    params = tuple((item.astype(jnp.float32) for item in (norm1_gain, norm1_bias, qkv_weight, qkv_bias, proj_weight, proj_bias, norm2_gain, norm2_bias, fc1_weight, fc1_bias, fc2_weight, fc2_bias)))
    row_count = tokens.shape[0] // ROW_LEN
    inputs_all = tokens.astype(jnp.float32).reshape(row_count, ROW_LEN, D)
    grads_all = cotangent.astype(jnp.float32).reshape(row_count, ROW_LEN, D)
    ids_all = picture_ids.reshape(row_count, ROW_LEN)
    place_all = positions.reshape(2, row_count, ROW_LEN).transpose(1, 0, 2)
    live_all = valid.reshape(row_count, ROW_LEN)

    def step(totals, packed):
        inputs, grad_out, picture, place, live = packed

        def forward(row_inputs, *weights):
            return row_forward(row_inputs, picture, place, live, *weights)
        result, pullback = jax.vjp(forward, inputs, *params)
        grads = pullback(grad_out)
        totals = tuple((first + second for first, second in zip(totals, grads[1:])))
        return (totals, (result, grads[0]))
    zeros = tuple((jnp.zeros_like(item) for item in params))
    totals, (results, input_grads) = lax.scan(step, zeros, (inputs_all, grads_all, ids_all, place_all, live_all))
    return (results.reshape(-1, D), input_grads.reshape(-1, D), totals[0], totals[1], totals[2], totals[3], totals[4], totals[5], totals[6], totals[7], totals[8], totals[9], totals[10], totals[11])
```

```python
import functools
import math

import jax
import jax.numpy as jnp
from jax import lax
from jax.experimental import pallas as pl
from jax.experimental.pallas import tpu as pltpu
from jax.sharding import PartitionSpec as P

HEAD_DIM = 80
EPS = 1e-06
LOG2E = math.log2(math.e)
FAR = 1e30
f32 = jnp.float32
bf16 = jnp.bfloat16
NT = (((1,), (1,)), ((), ()))
NN = (((1,), (0,)), ((), ()))
TN = (((0,), (0,)), ((), ()))


def lasts(micros):
    return pl.CostEstimate(flops=int(micros * 1.1e9), bytes_accessed=1, transcendentals=0)


ROOMY = pltpu.CompilerParams(vmem_limit_bytes=62 * 2**20)


def mm(left, right, dims):
    return lax.dot_general(left, right, dims, preferred_element_type=f32)


def whole(shape):
    return pl.BlockSpec(shape, lambda i: (0,) * len(shape))


def norm_parts(values):
    center = values - jnp.mean(values, axis=-1, keepdims=True)
    inverse = lax.rsqrt(jnp.mean(center * center, axis=-1, keepdims=True) + EPS)
    return center * inverse, inverse


def norm_backward(grad_out, unit, inverse, gain):
    scaled = grad_out * gain
    grad_in = inverse * (
        scaled
        - jnp.mean(scaled, axis=-1, keepdims=True)
        - unit * jnp.mean(scaled * unit, axis=-1, keepdims=True)
    )
    return (grad_in, jnp.sum(grad_out * unit, axis=0), jnp.sum(grad_out, axis=0))


def rope_tables(place, width):
    quarter = HEAD_DIM // 4
    freqs = 10000.0 ** (-2.0 * jnp.arange(quarter, dtype=f32) / (HEAD_DIM // 2))
    along_rows = place[0].astype(f32)[:, None] * freqs[None, :]
    along_cols = place[1].astype(f32)[:, None] * freqs[None, :]
    theta = jnp.concatenate([along_rows, along_cols], axis=1)
    lane = jnp.arange(width)[None, :] % HEAD_DIM
    entry = jnp.arange(HEAD_DIM // 2)[:, None]
    low = jnp.where(lane == entry, 1.0, 0.0)
    high = jnp.where(lane == entry + HEAD_DIM // 2, 1.0, 0.0)
    exact = functools.partial(jnp.dot, precision=lax.Precision.HIGHEST)
    cosine, sine = jnp.cos(theta), jnp.sin(theta)
    return exact(cosine, low + high), exact(sine, -low), exact(sine, high)


def mask_lanes(picture, valid, pairs):
    lane = jnp.arange(256)[None, None, :]
    pair = jnp.arange(pairs)[:, None, None]
    spare = (lane - 32 * pair - 160) % 256
    ident = picture[None, :, None]
    dead = (valid <= 0).astype(f32)[None, :, None]
    for_query = jnp.where(
        spare < 4, jnp.where(spare == ident, 0.0, -FAR), jnp.where(spare == 4, -FAR, 0.0)
    )
    for_key = jnp.where(
        spare < 4, jnp.where(spare == ident, 1.0, 0.0), jnp.where(spare == 4, dead, 0.0)
    )
    return for_query.astype(bf16), for_key.astype(bf16)


def window_lanes(pair):
    place = lax.broadcasted_iota(jnp.int32, (1, 256), 1) - 32 * pair
    first = (place >= 0) & (place < HEAD_DIM)
    second = (place >= HEAD_DIM) & (place < 2 * HEAD_DIM)
    return first, second, (place - 2 * HEAD_DIM) & 255


def as_ones(condition):
    return jnp.where(condition, 1.0, 0.0).astype(bf16)


def reach(length, block):
    half, most = length // 2, 3 * length // 4
    spans = []
    for start in range(0, length, block):
        if start + block <= half:
            spans.append((start, 0, most))
        elif start >= most:
            spans.append((start, half, length))
        else:
            spans.append((start, 0, length))
    return spans


def attend_kernel(*refs, block, begin):
    mq_ref, mk_ref, q_ref, k_ref, v_ref = refs[:5]
    o_ref, lse_ref, qs, ks, vs = refs[-5:]
    length = q_ref.shape[0]
    pair = pl.program_id(0) + begin
    if begin:

        @pl.when(pl.program_id(0) == 0)
        def _():
            o_ref[...] = refs[5][...]

    win = pl.ds(pl.multiple_of(128 * pair, 128), 256)
    first, second, spare = window_lanes(pair)
    both = first | second
    m0, m1, mp = as_ones(first), as_ones(second), as_ones(both)
    count0, count1 = as_ones(spare == 5), as_ones(spare == 6)
    for start in range(0, length, 512):
        rows = pl.ds(start, 512)
        mk = mk_ref[0, rows, :]
        k, v = k_ref[rows, win], v_ref[rows, win]
        qs[rows, :] = q_ref[rows, win] * mp + mq_ref[0, rows, :]
        ks[0, rows, :] = k * m0 + mk
        ks[1, rows, :] = k * m1 + mk
        vs[0, rows, :] = v * m0 + count0
        vs[1, rows, :] = v * m1 + count1
    for start, low, high in reach(length, block):
        rows, keys = pl.ds(start, block), pl.ds(low, high - low)
        weights, peaks = [], []
        for head in range(2):
            scores = mm(qs[rows, :], ks[head, keys, :], NT)
            peak = jnp.max(scores, axis=1, keepdims=True)
            peaks.append(peak)
            weights.append(jnp.exp2(scores - peak).astype(bf16))
        mixed = mm(
            jnp.concatenate(weights, 1),
            jnp.concatenate([vs[0, keys, :], vs[1, keys, :]], 0),
            NN,
        )
        total0 = jnp.sum(jnp.where(spare == 5, mixed, 0.0), axis=1, keepdims=True)
        total1 = jnp.sum(jnp.where(spare == 6, mixed, 0.0), axis=1, keepdims=True)
        mixed = mixed * jnp.where(first, 1.0 / total0, 1.0 / total1)
        o_ref[rows, win] = jnp.where(both, mixed, o_ref[rows, win].astype(f32)).astype(bf16)
        lane = lax.broadcasted_iota(jnp.int32, (block, 128), 1)
        sums = jnp.where(
            lane == 0,
            peaks[0] + jnp.log2(total0),
            jnp.where(lane == 1, peaks[1] + jnp.log2(total1), 0.0),
        )
        lse_ref[0, :, rows] = jnp.transpose(sums)[:8, :]


def attend(mq, mk, q, k, v, begin=0, count=None, before=(), block=512):
    length, width = q.shape
    count = mq.shape[0] - begin if count is None else count
    part = lambda shape, skip: pl.BlockSpec(shape, lambda i: (i + skip, 0, 0))
    return pl.pallas_call(
        functools.partial(attend_kernel, block=block, begin=begin),
        grid=(count,),
        in_specs=[part((1, length, 256), begin)] * 2
        + [whole((length, width))] * (3 + len(before)),
        out_specs=[whole((length, width)), part((1, 8, length), 0)],
        scratch_shapes=[pltpu.VMEM((length, 256), bf16)]
        + [pltpu.VMEM((2, length, 256), bf16)] * 2,
        out_shape=[
            jax.ShapeDtypeStruct((length, width), bf16),
            jax.ShapeDtypeStruct((count, 8, length), f32),
        ],
        compiler_params=ROOMY,
        cost_estimate=lasts(10),
        name="attend",
    )(mq, mk, q, k, v, *before)


def attend_back_kernel(
    mq_ref, mk_ref, q_ref, k_ref, v_ref, o_ref, g_ref, lse_ref, cos_ref, down_ref, up_ref,
    out_ref, qs, ks, gs, dq, center, *, block, step,
):
    length, width = q_ref.shape
    pair = pl.program_id(0)
    win = pl.ds(pl.multiple_of(128 * pair, 128), 256)
    first, second, _ = window_lanes(pair)
    both = first | second
    m0, m1 = as_ones(first), as_ones(second)
    row = lax.broadcasted_iota(jnp.int32, (8, 256), 0)
    pick = as_ones(((row == 0) & first) | ((row == 1) & second))
    for start in range(0, length, 512):
        rows = pl.ds(start, 512)
        mq, mk = mq_ref[0, rows, :], mk_ref[0, rows, :]
        q, k, g = q_ref[rows, win], k_ref[rows, win], g_ref[rows, win]
        qs[0, rows, :] = q * m0 + mq
        qs[1, rows, :] = q * m1 + mq
        ks[0, rows, :] = k * m0 + mk
        ks[1, rows, :] = k * m1 + mk
        gs[0, rows, :] = g * m0
        gs[1, rows, :] = g * m1
        product = g.astype(f32) * o_ref[rows, win].astype(f32)
        high = product.astype(bf16)
        low = (product - high.astype(f32)).astype(bf16)
        center[:, rows] = mm(pick, high, NT) + mm(pick, low, NT)
        dq[rows, :] = jnp.zeros((512, 256), f32)

    def turn_back(grad, rows):
        turned = (
            pltpu.roll(grad, 256 - HEAD_DIM // 2, 1) * down_ref[rows, win]
            + pltpu.roll(grad, HEAD_DIM // 2, 1) * up_ref[rows, win]
        )
        return grad * cos_ref[rows, win] - turned

    def put(grad, rows, part):
        to = pl.ds(pl.multiple_of(128 * pair + part * width, 128), 256)
        out_ref[rows, to] = jnp.where(both, grad, out_ref[rows, to].astype(f32)).astype(bf16)

    for start, low, high in reach(length, block):
        keys = pl.ds(start, block)
        v = v_ref[keys, win]
        dk = dv = None
        for at in range(low, high, step):
            rows = pl.ds(at, min(step, high - at))
            probs, grads = [], []
            for head in range(2):
                scores = mm(ks[head, keys, :], qs[head, rows, :], NT)
                prob_grad = mm(v, gs[head, rows, :], NT)
                prob = jnp.exp2(scores - lse_ref[0, head : head + 1, rows])
                probs.append(prob.astype(bf16))
                grads.append((prob * (prob_grad - center[head : head + 1, rows])).astype(bf16))
            dv_part = mm(
                jnp.concatenate(probs, 1),
                jnp.concatenate([gs[0, rows, :], gs[1, rows, :]], 0),
                NN,
            )
            dk_part = mm(
                jnp.concatenate(grads, 1),
                jnp.concatenate([qs[0, rows, :], qs[1, rows, :]], 0),
                NN,
            )
            dv = dv_part if dv is None else dv + dv_part
            dk = dk_part if dk is None else dk + dk_part
            dq[rows, :] += mm(
                jnp.concatenate(grads, 0),
                jnp.concatenate([ks[0, keys, :], ks[1, keys, :]], 0),
                TN,
            )
        put(turn_back(dk * (1.0 / LOG2E), keys), keys, 1)
        put(dv, keys, 2)
    for start in range(0, length, 512):
        rows = pl.ds(start, 512)
        put(turn_back(dq[rows, :] * HEAD_DIM**-0.5, rows), rows, 0)


def attend_back(mq, mk, q, k, v, o, g, lse, tables, block=512, step=1024):
    length, width = q.shape
    pairs = width // 128 - 1
    part = lambda shape: pl.BlockSpec(shape, lambda i: (i, 0, 0))
    return pl.pallas_call(
        functools.partial(attend_back_kernel, block=block, step=step),
        grid=(pairs,),
        in_specs=[part((1, length, 256))] * 2
        + [whole((length, width))] * 5
        + [part((1, 8, length))]
        + [whole((length, width))] * 3,
        out_specs=whole((length, 3 * width)),
        scratch_shapes=[pltpu.VMEM((2, length, 256), bf16)] * 3
        + [pltpu.VMEM((length, 256), f32), pltpu.VMEM((8, length), f32)],
        out_shape=jax.ShapeDtypeStruct((length, 3 * width), bf16),
        compiler_params=pltpu.CompilerParams(vmem_limit_bytes=63 * 2**20),
        cost_estimate=lasts(47),
        name="attend_back",
    )(mq, mk, q, k, v, o, g, lse, *tables)


def qkv_kernel(a, w, b, cos, down, up, q, k, v):
    width = q.shape[1]
    x = mm(a[...], w[...], NN) + b[...]

    def rotate(part):
        return (
            part * cos[...]
            + pltpu.roll(part, width - HEAD_DIM // 2, 1) * down[...]
            + pltpu.roll(part, HEAD_DIM // 2, 1) * up[...]
        )

    q[...] = (rotate(x[:, :width]) * (HEAD_DIM**-0.5 * LOG2E)).astype(bf16)
    k[...] = rotate(x[:, width : 2 * width]).astype(bf16)
    v[...] = x[:, 2 * width :].astype(bf16)


def qkv_rotate(a, w, b, tables, block=512):
    length, depth = a.shape
    width = w.shape[1] // 3
    rows = lambda n: pl.BlockSpec((block, n), lambda i: (i, 0))
    return pl.pallas_call(
        qkv_kernel,
        grid=(length // block,),
        in_specs=[rows(depth), whole(w.shape), whole(b.shape)] + [rows(width)] * 3,
        out_specs=[rows(width)] * 3,
        out_shape=[jax.ShapeDtypeStruct((length, width), bf16)] * 3,
        compiler_params=ROOMY,
        cost_estimate=lasts(9),
        name="qkv_rotate",
    )(a, w, b, *tables)


def hidden_kernel(c, w, b, hidden, slope):
    pre = mm(c[...], w[...], NN) + b[...]
    gate = 1.0 / (1.0 + jnp.exp2(pre * (-1.702 * LOG2E)))
    value = pre * gate
    hidden[...] = value.astype(bf16)
    slope[...] = (gate + 1.702 * value * (1.0 - gate)).astype(bf16)


def hidden_slope(c, w, b, block=128):
    length, depth = c.shape
    units = w.shape[1]
    rows = lambda n: pl.BlockSpec((block, n), lambda i: (i, 0))
    return pl.pallas_call(
        hidden_kernel,
        grid=(length // block,),
        in_specs=[rows(depth), whole(w.shape), whole(b.shape)],
        out_specs=[rows(units)] * 2,
        out_shape=[jax.ShapeDtypeStruct((length, units), bf16)] * 2,
        compiler_params=ROOMY,
        cost_estimate=lasts(7),
        name="hidden_slope",
    )(c, w, b)


def pre_grad_kernel(g, w, slope, out, bias):
    grad = (mm(g[...], w[...], NN) * slope[...].astype(f32)).astype(bf16)
    out[...] = grad

    @pl.when(pl.program_id(0) == 0)
    def _():
        bias[...] = jnp.zeros(bias.shape, f32)

    bias[...] += jnp.sum(grad.astype(f32).reshape(-1, 8, grad.shape[1]), axis=0)


def pre_grad(g, w, slope, block=256):
    length, depth = g.shape
    units = w.shape[1]
    rows = lambda n: pl.BlockSpec((block, n), lambda i: (i, 0))
    return pl.pallas_call(
        pre_grad_kernel,
        grid=(length // block,),
        in_specs=[rows(depth), whole(w.shape), rows(units)],
        out_specs=[rows(units), whole((8, units))],
        out_shape=[
            jax.ShapeDtypeStruct((length, units), bf16),
            jax.ShapeDtypeStruct((8, units), f32),
        ],
        compiler_params=ROOMY,
        cost_estimate=lasts(6),
        name="pre_grad",
    )(g, w, slope)


def weight_grad_kernel(*refs, count):
    total = None
    for left, right in zip(refs[:count], refs[count : 2 * count]):
        part = mm(left[...], right[...], TN)
        total = part if total is None else total + part
    refs[2 * count][...] = total.astype(bf16)


def weight_grad(lefts, rights, block=512):
    count = len(lefts)
    length, high = lefts[0].shape
    wide = rights[0].shape[1]
    if wide % block:
        block = 384 if wide % 384 == 0 else 128
    return pl.pallas_call(
        functools.partial(weight_grad_kernel, count=count),
        grid=(wide // block,),
        in_specs=[whole((length, high))] * count
        + [pl.BlockSpec((length, block), lambda i: (0, i))] * count,
        out_specs=pl.BlockSpec((high, block), lambda i: (0, i)),
        out_shape=jax.ShapeDtypeStruct((high, wide), bf16),
        compiler_params=ROOMY,
        cost_estimate=lasts(9),
        name="weight_grad",
    )(*lefts, *rights)


def flip(size, bit):
    return [(i, i ^ bit) for i in range(size)]


def send(value, pairs, axis="dp"):
    return lax.ppermute(value, axis, pairs)


def tie(*values):
    leaves, tree = jax.tree.flatten(values)
    return jax.tree.unflatten(tree, lax.optimization_barrier(leaves))


def gather_slow(shard, size):
    ring = size // 4
    pieces = [shard] + [
        send(shard, [(i, (i + 4 * step) % size) for i in range(size)]) for step in range(1, ring)
    ]
    return jnp.stack(pieces)


def gather_near(own, size):
    return send(own, flip(size, 1)), send(own, flip(size, 2))


def gather_far(near, size, cut):
    return send(near[0][:, :, :cut], flip(size, 2)), send(near[1][:, :, cut:], flip(size, 1))


def place_kernel(index_ref, own, fast, second, left, right, out, sem, *, size, cut):
    index = index_ref[0]
    high, low = index // 4, index % 4
    ring, rows = size // 4, own.shape[1]
    wide = out.shape[1]
    copies = []
    for piece, bits, start, stop in (
        (own, 0, 0, wide), (fast, 1, 0, wide), (second, 2, 0, wide),
        (left, 3, 0, cut), (right, 3, cut, wide),
    ):
        for step in range(ring):
            block = lax.rem(high - step + ring, ring) * 4 + (low ^ bits)
            to = out.at[pl.ds(pl.multiple_of(block * rows, rows), rows), pl.ds(start, stop - start)]
            copies.append(pltpu.make_async_copy(piece.at[step], to, sem.at[len(copies)]))
    for copy in copies:
        copy.start()
    for copy in copies:
        copy.wait()


def place(own, near, far, size):
    _, rows, wide = own.shape
    anywhere = pl.BlockSpec(memory_space=pl.ANY)
    return pl.pallas_call(
        functools.partial(place_kernel, size=size, cut=far[0].shape[2]),
        in_specs=[pl.BlockSpec(memory_space=pltpu.SMEM)] + [anywhere] * 5,
        out_specs=pl.BlockSpec(memory_space=pltpu.VMEM),
        scratch_shapes=[pltpu.SemaphoreType.DMA((5 * size // 4,))],
        out_shape=jax.ShapeDtypeStruct((rows * size, wide), bf16),
        compiler_params=pltpu.CompilerParams(vmem_limit_bytes=24 * 2**20),
        cost_estimate=lasts(1),
        name="place",
    )(lax.axis_index("dp").reshape(1), own, *near, *far)


def split_grad_kernel(*refs, count, size):
    index = refs[0][0]
    lefts, rights = refs[1 : 1 + count], refs[1 + count : 1 + 2 * count]
    outs, result = refs[1 + 2 * count : 5 + 2 * count], refs[5 + 2 * count]
    total = None
    for left, right in zip(lefts, rights):
        part = mm(left[...], right[...], TN)
        total = part if total is None else total + part
    result[...] = total.astype(bf16)
    high, low = index // 4, index % 4
    ring, rows = size // 4, outs[0].shape[1]
    for bits in range(4):
        for step in range(ring):
            block = lax.rem(high + step, ring) * 4 + (low ^ bits)
            outs[bits][step] = result[pl.ds(pl.multiple_of(block * rows, rows), rows), :]


def split_grad(lefts, rights, size, block=512):
    count = len(lefts)
    length, high = lefts[0].shape
    wide = rights[0].shape[1]
    ring, rows = size // 4, high // size
    return pl.pallas_call(
        functools.partial(split_grad_kernel, count=count, size=size),
        grid=(pl.cdiv(wide, block),),
        in_specs=[pl.BlockSpec(memory_space=pltpu.SMEM)]
        + [whole((length, high))] * count
        + [pl.BlockSpec((length, block), lambda i: (0, i))] * count,
        out_specs=[pl.BlockSpec((ring, rows, block), lambda i: (0, 0, i))] * 4,
        out_shape=[jax.ShapeDtypeStruct((ring, rows, wide), bf16)] * 4,
        scratch_shapes=[pltpu.VMEM((high, block), bf16)],
        compiler_params=ROOMY,
        cost_estimate=lasts(9),
        name="split_grad",
    )(lax.axis_index("dp").reshape(1), *lefts, *rights)


def add_low(*parts):
    total = parts[0].astype(f32)
    for part in parts[1:]:
        total = total + part.astype(f32)
    return total.astype(bf16)


def scatter_far(stacks, size, cut):
    far = stacks[3]
    return send(far[:, :, :cut], flip(size, 2)), send(far[:, :, cut:], flip(size, 1))


def scatter_near(stacks, got, size):
    left, right = got
    cut = left.shape[2]
    fast = jnp.concatenate([add_low(stacks[1][:, :, :cut], left), stacks[1][:, :, cut:]], axis=2)
    second = jnp.concatenate([stacks[2][:, :, :cut], add_low(stacks[2][:, :, cut:], right)], axis=2)
    return send(fast, flip(size, 1)), send(second, flip(size, 2))


def scatter_slow(stacks, got, size):
    total = add_low(stacks[0], *got)
    return total[0], [
        send(total[step], [(i, (i + 4 * step) % size) for i in range(size)])
        for step in range(1, size // 4)
    ]


def scatter_last(own, got):
    return sum((part.astype(f32) for part in got), own.astype(f32))


def sum_everywhere(value, size):
    for bit in [1 << i for i in range(size.bit_length() - 1)]:
        value = value + send(value, flip(size, bit))
    return value + send(value, [(0, 1), (1, 0)], "tensor")


def on_device(
    size,
    tokens,
    cotangent,
    picture_ids,
    positions,
    valid,
    norm1_gain,
    norm1_bias,
    qkv_weight,
    qkv_bias,
    proj_weight,
    proj_bias,
    norm2_gain,
    norm2_bias,
    fc1_weight,
    fc1_bias,
    fc2_weight,
    fc2_bias,
):
    me = lax.axis_index("tensor")
    length = picture_ids.shape[0]
    half, model = tokens.shape
    rows = qkv_weight.shape[0]
    width = qkv_weight.shape[2]
    units = fc1_weight.shape[1]
    swap = [(0, 1), (1, 0)]
    cross = lambda value: send(value, swap, "tensor")
    mine = lambda value: lax.dynamic_slice_in_dim(value, me * half, half, 0)
    theirs = lambda value: lax.dynamic_slice_in_dim(value, (1 - me) * half, half, 0)

    def in_order(own, other):
        return jnp.where(
            me == 0, jnp.concatenate([own, other], 0), jnp.concatenate([other, own], 0)
        )

    gain_one, shift_one = norm1_gain.astype(f32), norm1_bias.astype(f32)
    gain_two, shift_two = norm2_gain.astype(f32), norm2_bias.astype(f32)
    qkv_shift = lax.dynamic_slice_in_dim(qkv_bias.astype(f32), me * width, width, 1).reshape(1, -1)
    fc1_shift = lax.dynamic_slice_in_dim(fc1_bias.astype(f32), me * units, units, 0).reshape(1, -1)

    qkv_cut, cut, fc1_cut, fc2_cut = 1024, 1664, 1280, 1280
    inputs = tokens.astype(f32)
    unit_one, inverse_one = norm_parts(inputs)
    normed_own = (unit_one * gain_one + shift_one).astype(bf16)
    attn_in = in_order(normed_own, cross(normed_own))
    tables = rope_tables(positions, width)
    mq, mk = mask_lanes(picture_ids, valid, width // 128 - 1)

    qkv_own = gather_slow(qkv_weight.reshape(rows, 3 * width), size)
    joined = jnp.concatenate([proj_weight.T, fc1_weight], axis=1)
    qkv_own, joined = tie(qkv_own, joined)
    qkv_near = gather_near(qkv_own, size)
    own = gather_slow(joined, size)
    qkv_near, attn_in = tie(qkv_near, attn_in)
    qkv_far = gather_far(qkv_near, size, qkv_cut)
    qkv_far, own, tables = tie(qkv_far, own, tables)
    near = gather_near(own, size)
    qkv_full = place(qkv_own, qkv_near, qkv_far, size)
    q, k, v = qkv_rotate(attn_in, qkv_full, qkv_shift, tables)
    pairs = mq.shape[0]
    fc2_shard, q, mq = tie(fc2_weight.T, q, mq)
    fc2_own = gather_slow(fc2_shard, size)
    mixed, lse_low = attend(mq, mk, q, k, v, 0, pairs // 2)
    near, mixed = tie(near, mixed)
    far = gather_far(near, size, cut)
    mixed, lse_high = attend(mq, mk, q, k, v, pairs // 2, pairs - pairs // 2, (mixed,))
    far, fc2_own, mixed = tie(far, fc2_own, mixed)
    fc2_near = gather_near(fc2_own, size)
    joined = place(own, near, far, size)
    proj_turned, fc1_full = joined[:, :width], joined[:, width:]

    away = cross(mm(theirs(mixed), proj_turned, NT).astype(bf16))
    attn_out = mm(mine(mixed), proj_turned, NT) + away.astype(f32)
    middle = inputs + (attn_out + proj_bias.astype(f32))
    unit_two, inverse_two = norm_parts(middle)
    c_own = (unit_two * gain_two + shift_two).astype(bf16)
    grad_other = cross(cotangent)
    c_other = cross(c_own)
    hidden_own, slope_own = hidden_slope(c_own, fc1_full, fc1_shift)
    fc2_near, hidden_own = tie(fc2_near, hidden_own)
    fc2_far = gather_far(fc2_near, size, fc2_cut)
    hidden_other, slope_other = hidden_slope(c_other, fc1_full, fc1_shift)

    fc2_stacks = split_grad([cotangent, grad_other], [hidden_own, hidden_other], size)
    fc2_far, fc2_stacks = tie(fc2_far, fc2_stacks)
    fc2_got = scatter_far(fc2_stacks, size, fc2_cut)
    fc2_turned = place(fc2_own, fc2_near, fc2_far, size)
    pre_other, bias_other = pre_grad(grad_other, fc2_turned, slope_other)
    fc2_got, pre_other = tie(fc2_got, pre_other)
    fc2_got = scatter_near(fc2_stacks, fc2_got, size)
    pre_own, bias_own = pre_grad(cotangent, fc2_turned, slope_own)
    fc1_stacks = split_grad([c_own, c_other], [pre_own, pre_other], size)
    fc2_got, fc1_stacks, pre_other, pre_own = tie(fc2_got, fc1_stacks, pre_other, pre_own)
    fc2_kept, fc2_got = scatter_slow(fc2_stacks, fc2_got, size)
    fc1_got = scatter_far(fc1_stacks, size, fc1_cut)
    away = cross(mm(pre_other, fc1_full, NT).astype(bf16))
    normed_two_grad = mm(pre_own, fc1_full, NT) + away.astype(f32)

    out_grad = cotangent.astype(f32)
    fc2_shift_grad = jnp.sum(out_grad, axis=0)
    middle_part, gain_two_grad, shift_two_grad = norm_backward(
        normed_two_grad, unit_two, inverse_two, gain_two
    )
    middle_grad = out_grad + middle_part
    attn_grad_own = middle_grad.astype(bf16)
    proj_shift_grad = jnp.sum(attn_grad_own.astype(f32), axis=0)
    fc1_got, attn_grad_own = tie(fc1_got, attn_grad_own)
    attn_grad_other = cross(attn_grad_own)
    fc1_got = scatter_near(fc1_stacks, fc1_got, size)
    attn_grad = in_order(attn_grad_own, attn_grad_other)
    mixed_grad = mm(attn_grad, proj_turned, NN).astype(bf16)
    proj_grad = weight_grad([attn_grad], [mixed])
    fc1_got, fc2_got, mixed_grad, proj_grad = tie(fc1_got, fc2_got, mixed_grad, proj_grad)
    fc2_shard = scatter_last(fc2_kept, fc2_got)
    fc1_kept, fc1_got = scatter_slow(fc1_stacks, fc1_got, size)
    proj_shard = lax.psum_scatter(proj_grad, "dp", scatter_dimension=0, tiled=True).astype(f32)
    lse = jnp.concatenate([lse_low, lse_high], axis=0)
    mixed_grad, fc2_shard, fc1_kept = tie(mixed_grad, fc2_shard, fc1_kept)
    qkv_grad = attend_back(mq, mk, q, k, v, mixed, mixed_grad, lse, tables)
    fc1_got, proj_shard, qkv_grad = tie(fc1_got, proj_shard, qkv_grad)
    fc1_shard = scatter_last(fc1_kept, fc1_got)
    qkv_stacks = split_grad([attn_in], [qkv_grad], size)
    qkv_stacks, qkv_grad = tie(qkv_stacks, qkv_grad)
    qkv_got = scatter_far(qkv_stacks, size, qkv_cut)
    part = mm(theirs(qkv_grad), qkv_full, NT).astype(bf16)
    qkv_got, part = tie(qkv_got, part)
    qkv_got = scatter_near(qkv_stacks, qkv_got, size)
    normed_one_grad = mm(mine(qkv_grad), qkv_full, NT) + cross(part).astype(f32)
    qkv_shift_grad = jnp.sum(qkv_grad.astype(f32), axis=0)
    input_part, gain_one_grad, shift_one_grad = norm_backward(
        normed_one_grad, unit_one, inverse_one, gain_one
    )
    input_grad = middle_grad + input_part

    input_grad, hidden_other = tie(input_grad, hidden_other)
    part = mm(hidden_other, fc2_turned, NT).astype(bf16)
    qkv_got, part = tie(qkv_got, part)
    qkv_kept, qkv_got = scatter_slow(qkv_stacks, qkv_got, size)
    output = (
        middle + (mm(hidden_own, fc2_turned, NT) + cross(part).astype(f32)) + fc2_bias.astype(f32)
    )
    qkv_shard = scatter_last(qkv_kept, qkv_got)

    fc1_shift_grad = jnp.sum(bias_own, axis=0) + jnp.sum(bias_other, axis=0)
    fc1_place = lax.dynamic_update_slice_in_dim(
        jnp.zeros((2 * units,), f32), fc1_shift_grad, me * units, 0
    )
    qkv_place = lax.dynamic_update_slice_in_dim(
        jnp.zeros((3, 2 * width), f32), qkv_shift_grad.reshape(3, width), me * width, 1
    )
    sums = [
        gain_one_grad, shift_one_grad, qkv_place.reshape(-1), proj_shift_grad,
        gain_two_grad, shift_two_grad, fc1_place, fc2_shift_grad,
    ]
    totals = sum_everywhere(jnp.concatenate(sums).reshape(-1, 128), size).reshape(-1)
    small = []
    for part in sums:
        small.append(totals[: part.shape[0]])
        totals = totals[part.shape[0] :]
    return (
        output,
        input_grad,
        small[0],
        small[1],
        qkv_shard.reshape(rows, 3, width),
        small[2].reshape(3, 2 * width),
        proj_shard.T,
        small[3],
        small[4],
        small[5],
        fc1_shard,
        small[6],
        fc2_shard.T,
        small[7],
    )


def norm_forward(values, gain, shift):
    center = values - jnp.mean(values, axis=-1, keepdims=True)
    inverse = lax.rsqrt(jnp.mean(center * center, axis=-1, keepdims=True) + EPS)
    unit = center * inverse
    return (unit * gain + shift, unit, inverse)


def on_any(
    tokens,
    cotangent,
    picture_ids,
    positions,
    valid,
    norm1_gain,
    norm1_bias,
    qkv_weight,
    qkv_bias,
    proj_weight,
    proj_bias,
    norm2_gain,
    norm2_bias,
    fc1_weight,
    fc1_bias,
    fc2_weight,
    fc2_bias,
):
    tensor_index = lax.axis_index("tensor")
    model_width = tokens.shape[1]
    local_width = qkv_weight.shape[2]
    local_hidden = fc1_weight.shape[1]
    local_heads = local_width // HEAD_DIM
    gain_one = norm1_gain.astype(jnp.float32)
    shift_one = norm1_bias.astype(jnp.float32)
    gain_two = norm2_gain.astype(jnp.float32)
    shift_two = norm2_bias.astype(jnp.float32)
    qkv_shift = lax.dynamic_slice_in_dim(
        qkv_bias.astype(jnp.float32), tensor_index * local_width, local_width, 1
    ).reshape(3 * local_width)
    fc1_shift = lax.dynamic_slice_in_dim(
        fc1_bias.astype(jnp.float32), tensor_index * local_hidden, local_hidden, 0
    )
    qkv_full, proj_full, fc1_full, fc2_full = (
        lax.all_gather(qkv_weight, "dp", axis=0, tiled=True),
        lax.all_gather(proj_weight, "dp", axis=1, tiled=True),
        lax.all_gather(fc1_weight, "dp", axis=0, tiled=True),
        lax.all_gather(fc2_weight, "dp", axis=1, tiled=True),
    )
    qkv_matrix = qkv_full.reshape(model_width, 3 * local_width)
    inputs = tokens.astype(jnp.float32)
    normed_one, unit_one, inverse_one = norm_forward(inputs, gain_one, shift_one)
    attn_in = lax.all_gather(normed_one.astype(jnp.bfloat16), "tensor", axis=0, tiled=True)
    total_rows = attn_in.shape[0]
    qkv_raw = jnp.dot(attn_in, qkv_matrix, preferred_element_type=jnp.float32) + qkv_shift
    pairs = -(-local_heads // 2)
    padded = 128 * (pairs + 1)
    fill = lambda value: jnp.pad(value, ((0, 0), (0, padded - local_width)))
    tables = [fill(table) for table in rope_tables(positions, local_width)]
    mq, mk = mask_lanes(picture_ids, valid, pairs)

    def rotate(part):
        turned = jnp.roll(part, -HEAD_DIM // 2, 1) * tables[1]
        return part * tables[0] + turned + jnp.roll(part, HEAD_DIM // 2, 1) * tables[2]

    split = [fill(part) for part in jnp.split(qkv_raw, 3, axis=1)]
    queries = (rotate(split[0]) * (HEAD_DIM**-0.5 * LOG2E)).astype(jnp.bfloat16)
    keys = rotate(split[1]).astype(jnp.bfloat16)
    values = split[2].astype(jnp.bfloat16)
    mixed_row, logsum_row = attend(mq, mk, queries, keys, values)
    attn_mixed = mixed_row[:, :local_width]
    piece = attn_mixed
    attn_out = lax.psum_scatter(
        jnp.dot(piece, proj_full, preferred_element_type=jnp.float32).astype(jnp.bfloat16),
        "tensor",
        scatter_dimension=0,
        tiled=True,
    ).astype(jnp.float32) + proj_bias.astype(jnp.float32)
    middle = inputs + attn_out
    normed_two, unit_two, inverse_two = norm_forward(middle, gain_two, shift_two)
    mlp_in = lax.all_gather(normed_two.astype(jnp.bfloat16), "tensor", axis=0, tiled=True)
    hidden_pre = jnp.dot(mlp_in, fc1_full, preferred_element_type=jnp.float32) + fc1_shift
    sigmoid_gate = jax.nn.sigmoid(1.702 * hidden_pre)
    hidden = (hidden_pre * sigmoid_gate).astype(jnp.bfloat16)
    piece = hidden
    mlp_out = lax.psum_scatter(
        jnp.dot(piece, fc2_full, preferred_element_type=jnp.float32).astype(jnp.bfloat16),
        "tensor",
        scatter_dimension=0,
        tiled=True,
    ).astype(jnp.float32) + fc2_bias.astype(jnp.float32)
    output = middle + mlp_out
    qkv_back, proj_back, fc1_back, fc2_back = (
        lax.all_gather(qkv_weight, "dp", axis=0, tiled=True),
        lax.all_gather(proj_weight, "dp", axis=1, tiled=True),
        lax.all_gather(fc1_weight, "dp", axis=0, tiled=True),
        lax.all_gather(fc2_weight, "dp", axis=1, tiled=True),
    )
    qkv_back = qkv_back.reshape(model_width, 3 * local_width)
    out_grad = cotangent.astype(jnp.float32)
    fc2_shift_grad = jnp.sum(out_grad, axis=0)
    out_grad_full = lax.all_gather(cotangent, "tensor", axis=0, tiled=True)
    fc2_grad = jnp.dot(hidden.T, out_grad_full, preferred_element_type=jnp.float32)
    hidden_grad = jnp.dot(out_grad_full, fc2_back.T, preferred_element_type=jnp.float32)
    slope = sigmoid_gate + 1.702 * hidden_pre * sigmoid_gate * (1.0 - sigmoid_gate)
    pre_grad = (hidden_grad * slope).astype(jnp.bfloat16)
    fc1_shift_grad = jnp.sum(pre_grad.astype(jnp.float32), axis=0)
    fc1_grad = jnp.dot(mlp_in.T, pre_grad, preferred_element_type=jnp.float32)
    piece = pre_grad
    normed_two_grad = lax.psum_scatter(
        jnp.dot(piece, fc1_back.T, preferred_element_type=jnp.float32).astype(jnp.bfloat16),
        "tensor",
        scatter_dimension=0,
        tiled=True,
    ).astype(jnp.float32)
    middle_part, gain_two_grad, shift_two_grad = norm_backward(
        normed_two_grad, unit_two, inverse_two, gain_two
    )
    middle_grad = out_grad + middle_part
    attn_grad_low = middle_grad.astype(jnp.bfloat16)
    proj_shift_grad = jnp.sum(attn_grad_low.astype(jnp.float32), axis=0)
    attn_grad_full = lax.all_gather(attn_grad_low, "tensor", axis=0, tiled=True)
    proj_grad = jnp.dot(attn_mixed.T, attn_grad_full, preferred_element_type=jnp.float32)
    mixed_grad = jnp.dot(attn_grad_full, proj_back.T, preferred_element_type=jnp.float32).astype(
        jnp.bfloat16
    )
    qkv_grad = attend_back(
        mq, mk, queries, keys, values, mixed_row, fill(mixed_grad), logsum_row, tables
    )
    qkv_grad = jnp.concatenate(
        [qkv_grad[:, at : at + local_width] for at in (0, padded, 2 * padded)], axis=1
    )
    qkv_shift_grad = jnp.sum(qkv_grad.astype(jnp.float32), axis=0)
    qkv_grad_weight = jnp.dot(attn_in.T, qkv_grad, preferred_element_type=jnp.float32)
    qkv_grad_weight = qkv_grad_weight.reshape(model_width, 3, local_width)
    piece = qkv_grad
    normed_one_grad = lax.psum_scatter(
        jnp.dot(piece, qkv_back.T, preferred_element_type=jnp.float32).astype(jnp.bfloat16),
        "tensor",
        scatter_dimension=0,
        tiled=True,
    ).astype(jnp.float32)
    input_part, gain_one_grad, shift_one_grad = norm_backward(
        normed_one_grad, unit_one, inverse_one, gain_one
    )
    input_grad = middle_grad + input_part
    qkv_grad_shard, proj_grad_shard, fc1_grad_shard, fc2_grad_shard = (
        lax.psum_scatter(
            qkv_grad_weight.astype(jnp.bfloat16), "dp", scatter_dimension=0, tiled=True
        ).astype(jnp.float32),
        lax.psum_scatter(
            proj_grad.astype(jnp.bfloat16), "dp", scatter_dimension=1, tiled=True
        ).astype(jnp.float32),
        lax.psum_scatter(
            fc1_grad.astype(jnp.bfloat16), "dp", scatter_dimension=0, tiled=True
        ).astype(jnp.float32),
        lax.psum_scatter(
            fc2_grad.astype(jnp.bfloat16), "dp", scatter_dimension=1, tiled=True
        ).astype(jnp.float32),
    )
    qkv_shift_full = lax.dynamic_update_slice_in_dim(
        jnp.zeros((3, model_width), jnp.float32),
        qkv_shift_grad.reshape(3, local_width),
        tensor_index * local_width,
        1,
    )
    fc1_shift_full = lax.dynamic_update_slice_in_dim(
        jnp.zeros((fc1_bias.shape[0],), jnp.float32), fc1_shift_grad, tensor_index * local_hidden, 0
    )
    summed = lax.psum(
        (
            gain_one_grad,
            shift_one_grad,
            qkv_shift_full,
            proj_shift_grad,
            gain_two_grad,
            shift_two_grad,
            fc1_shift_full,
            fc2_shift_grad,
        ),
        ("dp", "tensor"),
    )
    return (
        output,
        input_grad,
        summed[0],
        summed[1],
        qkv_grad_shard,
        summed[2],
        proj_grad_shard,
        summed[3],
        summed[4],
        summed[5],
        fc1_grad_shard,
        summed[6],
        fc2_grad_shard,
        summed[7],
    )


def solution(mesh):
    size = mesh.shape["dp"]
    paired = mesh.shape["tensor"] == 2 and size == 16
    return jax.shard_map(
        functools.partial(on_device, size) if paired else on_any,
        mesh=mesh,
        in_specs=(
            P(("dp", "tensor"), None),
            P(("dp", "tensor"), None),
            P("dp"),
            P(None, "dp"),
            P("dp"),
            P(),
            P(),
            P("dp", None, "tensor"),
            P(),
            P("tensor", "dp"),
            P(),
            P(),
            P(),
            P("dp", "tensor"),
            P(),
            P("tensor", "dp"),
            P(),
        ),
        out_specs=(
            P(("dp", "tensor"), None),
            P(("dp", "tensor"), None),
            P(),
            P(),
            P("dp", None, "tensor"),
            P(),
            P("tensor", "dp"),
            P(),
            P(),
            P(),
            P("dp", "tensor"),
            P(),
            P("tensor", "dp"),
            P(),
        ),
        check_vma=False,
    )
```

```python
import functools
import math

import jax
import jax.numpy as jnp
from jax import lax
from jax.experimental import pallas as pl
from jax.experimental.pallas import tpu as pltpu
from jax.sharding import PartitionSpec as P

HEAD_DIM = 80
EPS = 1e-06
LOG2E = math.log2(math.e)
FAR = 1e30
f32 = jnp.float32
bf16 = jnp.bfloat16
NT = (((1,), (1,)), ((), ()))
NN = (((1,), (0,)), ((), ()))
TN = (((0,), (0,)), ((), ()))


INSTANT = pl.CostEstimate(flops=1, bytes_accessed=1, transcendentals=0)
ROOMY = pltpu.CompilerParams(vmem_limit_bytes=62 * 2**20)


def mm(left, right, dims):
    return lax.dot_general(left, right, dims, preferred_element_type=f32)


def whole(shape):
    return pl.BlockSpec(shape, lambda i: (0,) * len(shape))


def norm_parts(values):
    center = values - jnp.mean(values, axis=-1, keepdims=True)
    inverse = lax.rsqrt(jnp.mean(center * center, axis=-1, keepdims=True) + EPS)
    return center * inverse, inverse


def norm_backward(grad_out, unit, inverse, gain):
    scaled = grad_out * gain
    grad_in = inverse * (
        scaled
        - jnp.mean(scaled, axis=-1, keepdims=True)
        - unit * jnp.mean(scaled * unit, axis=-1, keepdims=True)
    )
    return (grad_in, jnp.sum(grad_out * unit, axis=0), jnp.sum(grad_out, axis=0))


def rope_tables(place, width):
    quarter = HEAD_DIM // 4
    freqs = 10000.0 ** (-2.0 * jnp.arange(quarter, dtype=f32) / (HEAD_DIM // 2))
    along_rows = place[0].astype(f32)[:, None] * freqs[None, :]
    along_cols = place[1].astype(f32)[:, None] * freqs[None, :]
    theta = jnp.concatenate([along_rows, along_cols], axis=1)
    lane = jnp.arange(width)[None, :] % HEAD_DIM
    entry = jnp.arange(HEAD_DIM // 2)[:, None]
    low = jnp.where(lane == entry, 1.0, 0.0)
    high = jnp.where(lane == entry + HEAD_DIM // 2, 1.0, 0.0)
    exact = functools.partial(jnp.dot, precision=lax.Precision.HIGHEST)
    cosine, sine = jnp.cos(theta), jnp.sin(theta)
    return exact(cosine, low + high), exact(sine, -low), exact(sine, high)


def mask_lanes(picture, valid, pairs):
    lane = jnp.arange(256)[None, None, :]
    pair = jnp.arange(pairs)[:, None, None]
    spare = (lane - 32 * pair - 160) % 256
    ident = picture[None, :, None]
    dead = (valid <= 0).astype(f32)[None, :, None]
    for_query = jnp.where(
        spare < 4, jnp.where(spare == ident, 0.0, -FAR), jnp.where(spare == 4, -FAR, 0.0)
    )
    for_key = jnp.where(
        spare < 4, jnp.where(spare == ident, 1.0, 0.0), jnp.where(spare == 4, dead, 0.0)
    )
    return for_query.astype(bf16), for_key.astype(bf16)


def window_lanes(pair):
    place = lax.broadcasted_iota(jnp.int32, (1, 256), 1) - 32 * pair
    first = (place >= 0) & (place < HEAD_DIM)
    second = (place >= HEAD_DIM) & (place < 2 * HEAD_DIM)
    return first, second, (place - 2 * HEAD_DIM) & 255


def as_ones(condition):
    return jnp.where(condition, 1.0, 0.0).astype(bf16)


def reach(length, block):
    half, most = length // 2, 3 * length // 4
    spans = []
    for start in range(0, length, block):
        if start + block <= half:
            spans.append((start, 0, most))
        elif start >= most:
            spans.append((start, half, length))
        else:
            spans.append((start, 0, length))
    return spans


def attend_kernel(*refs, block, begin):
    mq_ref, mk_ref, q_ref, k_ref, v_ref = refs[:5]
    o_ref, lse_ref, qs, ks, vs = refs[-5:]
    length = q_ref.shape[0]
    pair = pl.program_id(0) + begin
    if begin:

        @pl.when(pl.program_id(0) == 0)
        def _():
            o_ref[...] = refs[5][...]

    win = pl.ds(pl.multiple_of(128 * pair, 128), 256)
    first, second, spare = window_lanes(pair)
    both = first | second
    m0, m1, mp = as_ones(first), as_ones(second), as_ones(both)
    count0, count1 = as_ones(spare == 5), as_ones(spare == 6)
    for start in range(0, length, 512):
        rows = pl.ds(start, 512)
        mk = mk_ref[0, rows, :]
        k, v = k_ref[rows, win], v_ref[rows, win]
        qs[rows, :] = q_ref[rows, win] * mp + mq_ref[0, rows, :]
        ks[0, rows, :] = k * m0 + mk
        ks[1, rows, :] = k * m1 + mk
        vs[0, rows, :] = v * m0 + count0
        vs[1, rows, :] = v * m1 + count1
    for start, low, high in reach(length, block):
        rows, keys = pl.ds(start, block), pl.ds(low, high - low)
        weights, peaks = [], []
        for head in range(2):
            scores = mm(qs[rows, :], ks[head, keys, :], NT)
            peak = jnp.max(scores, axis=1, keepdims=True)
            peaks.append(peak)
            weights.append(jnp.exp2(scores - peak).astype(bf16))
        mixed = mm(
            jnp.concatenate(weights, 1),
            jnp.concatenate([vs[0, keys, :], vs[1, keys, :]], 0),
            NN,
        )
        total0 = jnp.sum(jnp.where(spare == 5, mixed, 0.0), axis=1, keepdims=True)
        total1 = jnp.sum(jnp.where(spare == 6, mixed, 0.0), axis=1, keepdims=True)
        mixed = mixed * jnp.where(first, 1.0 / total0, 1.0 / total1)
        o_ref[rows, win] = jnp.where(both, mixed, o_ref[rows, win].astype(f32)).astype(bf16)
        lane = lax.broadcasted_iota(jnp.int32, (block, 128), 1)
        sums = jnp.where(
            lane == 0,
            peaks[0] + jnp.log2(total0),
            jnp.where(lane == 1, peaks[1] + jnp.log2(total1), 0.0),
        )
        lse_ref[0, :, rows] = jnp.transpose(sums)[:8, :]


def attend(mq, mk, q, k, v, begin=0, count=None, before=(), block=512):
    length, width = q.shape
    count = mq.shape[0] - begin if count is None else count
    part = lambda shape, skip: pl.BlockSpec(shape, lambda i: (i + skip, 0, 0))
    return pl.pallas_call(
        functools.partial(attend_kernel, block=block, begin=begin),
        grid=(count,),
        in_specs=[part((1, length, 256), begin)] * 2
        + [whole((length, width))] * (3 + len(before)),
        out_specs=[whole((length, width)), part((1, 8, length), 0)],
        scratch_shapes=[pltpu.VMEM((length, 256), bf16)]
        + [pltpu.VMEM((2, length, 256), bf16)] * 2,
        out_shape=[
            jax.ShapeDtypeStruct((length, width), bf16),
            jax.ShapeDtypeStruct((count, 8, length), f32),
        ],
        compiler_params=ROOMY,
        cost_estimate=INSTANT,
        name="attend",
    )(mq, mk, q, k, v, *before)


def attend_back_kernel(
    mq_ref, mk_ref, q_ref, k_ref, v_ref, o_ref, g_ref, lse_ref, cos_ref, down_ref, up_ref,
    out_ref, qs, ks, gs, dq, center, *, block, step,
):
    length, width = q_ref.shape
    pair = pl.program_id(0)
    win = pl.ds(pl.multiple_of(128 * pair, 128), 256)
    first, second, _ = window_lanes(pair)
    both = first | second
    m0, m1 = as_ones(first), as_ones(second)
    row = lax.broadcasted_iota(jnp.int32, (8, 256), 0)
    pick = as_ones(((row == 0) & first) | ((row == 1) & second))
    for start in range(0, length, 512):
        rows = pl.ds(start, 512)
        mq, mk = mq_ref[0, rows, :], mk_ref[0, rows, :]
        q, k, g = q_ref[rows, win], k_ref[rows, win], g_ref[rows, win]
        qs[0, rows, :] = q * m0 + mq
        qs[1, rows, :] = q * m1 + mq
        ks[0, rows, :] = k * m0 + mk
        ks[1, rows, :] = k * m1 + mk
        gs[0, rows, :] = g * m0
        gs[1, rows, :] = g * m1
        product = g.astype(f32) * o_ref[rows, win].astype(f32)
        high = product.astype(bf16)
        low = (product - high.astype(f32)).astype(bf16)
        center[:, rows] = mm(pick, high, NT) + mm(pick, low, NT)
        dq[rows, :] = jnp.zeros((512, 256), f32)

    def turn_back(grad, rows):
        turned = (
            pltpu.roll(grad, 256 - HEAD_DIM // 2, 1) * down_ref[rows, win]
            + pltpu.roll(grad, HEAD_DIM // 2, 1) * up_ref[rows, win]
        )
        return grad * cos_ref[rows, win] - turned

    def put(grad, rows, part):
        to = pl.ds(pl.multiple_of(128 * pair + part * width, 128), 256)
        out_ref[rows, to] = jnp.where(both, grad, out_ref[rows, to].astype(f32)).astype(bf16)

    for start, low, high in reach(length, block):
        keys = pl.ds(start, block)
        v = v_ref[keys, win]
        dk = dv = None
        for at in range(low, high, step):
            rows = pl.ds(at, min(step, high - at))
            probs, grads = [], []
            for head in range(2):
                scores = mm(ks[head, keys, :], qs[head, rows, :], NT)
                prob_grad = mm(v, gs[head, rows, :], NT)
                prob = jnp.exp2(scores - lse_ref[0, head : head + 1, rows])
                probs.append(prob.astype(bf16))
                grads.append((prob * (prob_grad - center[head : head + 1, rows])).astype(bf16))
            dv_part = mm(
                jnp.concatenate(probs, 1),
                jnp.concatenate([gs[0, rows, :], gs[1, rows, :]], 0),
                NN,
            )
            dk_part = mm(
                jnp.concatenate(grads, 1),
                jnp.concatenate([qs[0, rows, :], qs[1, rows, :]], 0),
                NN,
            )
            dv = dv_part if dv is None else dv + dv_part
            dk = dk_part if dk is None else dk + dk_part
            dq[rows, :] += mm(
                jnp.concatenate(grads, 0),
                jnp.concatenate([ks[0, keys, :], ks[1, keys, :]], 0),
                TN,
            )
        put(turn_back(dk * (1.0 / LOG2E), keys), keys, 1)
        put(dv, keys, 2)
    for start in range(0, length, 512):
        rows = pl.ds(start, 512)
        put(turn_back(dq[rows, :] * HEAD_DIM**-0.5, rows), rows, 0)


def attend_back(mq, mk, q, k, v, o, g, lse, tables, block=512, step=1024):
    length, width = q.shape
    pairs = width // 128 - 1
    part = lambda shape: pl.BlockSpec(shape, lambda i: (i, 0, 0))
    return pl.pallas_call(
        functools.partial(attend_back_kernel, block=block, step=step),
        grid=(pairs,),
        in_specs=[part((1, length, 256))] * 2
        + [whole((length, width))] * 5
        + [part((1, 8, length))]
        + [whole((length, width))] * 3,
        out_specs=whole((length, 3 * width)),
        scratch_shapes=[pltpu.VMEM((2, length, 256), bf16)] * 3
        + [pltpu.VMEM((length, 256), f32), pltpu.VMEM((8, length), f32)],
        out_shape=jax.ShapeDtypeStruct((length, 3 * width), bf16),
        compiler_params=pltpu.CompilerParams(vmem_limit_bytes=63 * 2**20),
        cost_estimate=INSTANT,
        name="attend_back",
    )(mq, mk, q, k, v, o, g, lse, *tables)


def qkv_kernel(where, own, other, w, b, cos, down, up, q, k, v):
    width = q.shape[1]
    mine = pl.program_id(0) // (pl.num_programs(0) // 2) == where[0]
    x = mm(jnp.where(mine, own[...], other[...]), w[...], NN) + b[...]

    def rotate(part):
        return (
            part * cos[...]
            + pltpu.roll(part, width - HEAD_DIM // 2, 1) * down[...]
            + pltpu.roll(part, HEAD_DIM // 2, 1) * up[...]
        )

    q[...] = (rotate(x[:, :width]) * (HEAD_DIM**-0.5 * LOG2E)).astype(bf16)
    k[...] = rotate(x[:, width : 2 * width]).astype(bf16)
    v[...] = x[:, 2 * width :].astype(bf16)


def qkv_rotate(where, own, other, w, b, tables, block=512):
    half, depth = own.shape
    width = w.shape[1] // 3
    steps = half // block
    rows = lambda n: pl.BlockSpec((block, n), lambda i, w: (i, 0))
    part = pl.BlockSpec((block, depth), lambda i, w: (i % steps, 0))
    fixed = lambda shape: pl.BlockSpec(shape, lambda i, w: (0, 0))
    return pl.pallas_call(
        qkv_kernel,
        grid_spec=pltpu.PrefetchScalarGridSpec(
            num_scalar_prefetch=1,
            grid=(2 * steps,),
            in_specs=[part, part, fixed(w.shape), fixed(b.shape)] + [rows(width)] * 3,
            out_specs=[rows(width)] * 3,
        ),
        out_shape=[jax.ShapeDtypeStruct((2 * half, width), bf16)] * 3,
        compiler_params=ROOMY,
        cost_estimate=INSTANT,
        name="qkv_rotate",
    )(where, own, other, w, b, *tables)


def hidden_kernel(c, w, b, hidden, slope):
    pre = mm(c[...], w[...], NN) + b[...]
    gate = 1.0 / (1.0 + jnp.exp2(pre * (-1.702 * LOG2E)))
    value = pre * gate
    hidden[...] = value.astype(bf16)
    slope[...] = (gate + 1.702 * value * (1.0 - gate)).astype(bf16)


def hidden_slope(c, w, b, block=128):
    length, depth = c.shape
    units = w.shape[1]
    rows = lambda n: pl.BlockSpec((block, n), lambda i: (i, 0))
    return pl.pallas_call(
        hidden_kernel,
        grid=(length // block,),
        in_specs=[rows(depth), whole(w.shape), whole(b.shape)],
        out_specs=[rows(units)] * 2,
        out_shape=[jax.ShapeDtypeStruct((length, units), bf16)] * 2,
        compiler_params=ROOMY,
        cost_estimate=INSTANT,
        name="hidden_slope",
    )(c, w, b)


def pre_grad_kernel(g, w, slope, out, bias):
    grad = (mm(g[...], w[...], NN) * slope[...].astype(f32)).astype(bf16)
    out[...] = grad

    @pl.when(pl.program_id(0) == 0)
    def _():
        bias[...] = jnp.zeros(bias.shape, f32)

    bias[...] += jnp.sum(grad.astype(f32).reshape(-1, 8, grad.shape[1]), axis=0)


def pre_grad(g, w, slope, block=256):
    length, depth = g.shape
    units = w.shape[1]
    rows = lambda n: pl.BlockSpec((block, n), lambda i: (i, 0))
    return pl.pallas_call(
        pre_grad_kernel,
        grid=(length // block,),
        in_specs=[rows(depth), whole(w.shape), rows(units)],
        out_specs=[rows(units), whole((8, units))],
        out_shape=[
            jax.ShapeDtypeStruct((length, units), bf16),
            jax.ShapeDtypeStruct((8, units), f32),
        ],
        compiler_params=ROOMY,
        cost_estimate=INSTANT,
        name="pre_grad",
    )(g, w, slope)


def weight_grad_kernel(*refs, count, size):
    where = refs[0]
    lefts, rights = refs[1 : 1 + count], refs[1 + count : 1 + 2 * count]
    outs = refs[1 + 2 * count :]
    total = None
    for left, right in zip(lefts, rights):
        part = mm(left[...], right[...], TN)
        total = part if total is None else total + part
    if not size:
        outs[0][...] = total.astype(bf16)
        return
    result = outs[-1]
    result[...] = total.astype(bf16)
    index = where[1]
    high, low = index // 4, index % 4
    ring, rows = size // 4, outs[0].shape[1]
    for out, order in zip(outs, scatter_order(ring)):
        for slot, (bits, step) in enumerate(order):
            block = lax.rem(high + step, ring) * 4 + (low ^ bits)
            out[slot] = result[pl.ds(pl.multiple_of(block * rows, rows), rows), :]


def weight_grad(where, lefts, rights, size=0, block=512):
    length, high = lefts[0].shape
    wide = rights[0].shape[1]
    if len(rights) == 1:
        rights = rights * 2
        specs = [
            pl.BlockSpec((length, block), lambda i, w: (w[0], i)),
            pl.BlockSpec((length, block), lambda i, w: (1 - w[0], i)),
        ]
    else:
        specs = [pl.BlockSpec((length, block), lambda i, w: (0, i))] * 2
    if size:
        stacks = [(len(order), high // size) for order in scatter_order(size // 4)]
        out_specs = [pl.BlockSpec(stack + (block,), lambda i, w: (0, 0, i)) for stack in stacks]
        out_shape = [jax.ShapeDtypeStruct(stack + (wide,), bf16) for stack in stacks]
        scratch = [pltpu.VMEM((high, block), bf16)]
    else:
        out_specs = pl.BlockSpec((high, block), lambda i, w: (0, i))
        out_shape = jax.ShapeDtypeStruct((high, wide), bf16)
        scratch = []
    return pl.pallas_call(
        functools.partial(weight_grad_kernel, count=2, size=size),
        grid_spec=pltpu.PrefetchScalarGridSpec(
            num_scalar_prefetch=1,
            grid=(pl.cdiv(wide, block),),
            in_specs=[pl.BlockSpec((length, high), lambda i, w: (0, 0))] * 2 + specs,
            out_specs=out_specs,
            scratch_shapes=scratch,
        ),
        out_shape=out_shape,
        compiler_params=ROOMY,
        cost_estimate=INSTANT,
        name="weight_grad",
    )(where, *lefts, *rights)


def mixed_grad_kernel(where, own, other, w, out):
    value = jnp.where(pl.program_id(0) < pl.num_programs(0) // 2, own[...], other[...])
    out[...] = mm(value, w[...], NN).astype(bf16)


def mixed_grad_rows(where, own, other, w, block=512):
    half, depth = own.shape
    wide = w.shape[1]
    steps = half // block
    return pl.pallas_call(
        mixed_grad_kernel,
        grid_spec=pltpu.PrefetchScalarGridSpec(
            num_scalar_prefetch=1,
            grid=(2 * steps,),
            in_specs=[
                pl.BlockSpec((block, depth), lambda i, w: (jnp.minimum(i, steps - 1), 0)),
                pl.BlockSpec((block, depth), lambda i, w: (jnp.maximum(i - steps, 0), 0)),
                pl.BlockSpec((depth, wide), lambda i, w: (0, 0)),
            ],
            out_specs=pl.BlockSpec(
                (block, wide), lambda i, w: ((w[0] * steps + i) % (2 * steps), 0)
            ),
        ),
        out_shape=jax.ShapeDtypeStruct((2 * half, wide), bf16),
        compiler_params=ROOMY,
        cost_estimate=INSTANT,
        name="mixed_grad",
    )(where, own, other, w)


def closing_kernel(*refs, finish, extras, outs):
    x, w = refs[1:3]
    given = [ref[...] for ref in refs[3 : 3 + extras]]
    results, sums = finish(mm(x[...], w[...], NT), *given)
    for ref, value in zip(refs[3 + extras : 3 + extras + outs], results):
        ref[...] = value.astype(ref.dtype)
    totals = refs[3 + extras + outs :]

    @pl.when(pl.program_id(0) == 0)
    def _():
        for ref in totals:
            ref[...] = jnp.zeros(ref.shape, f32)

    for ref, value in zip(totals, sums):
        ref[...] += jnp.sum(value.reshape(-1, 8, value.shape[1]), axis=0)


def closing(where, x, w, rows, vectors, finish, kinds, sums, name, block=256):
    half, model = rows[0].shape
    depth = x.shape[1]
    steps = half // block
    skip = x.shape[0] > half
    part = pl.BlockSpec((block, model), lambda i, w: (i, 0))
    fixed = lambda shape: pl.BlockSpec(shape, lambda i, w: (0, 0))
    results = pl.pallas_call(
        functools.partial(
            closing_kernel, finish=finish, extras=len(rows) + len(vectors), outs=len(kinds)
        ),
        grid_spec=pltpu.PrefetchScalarGridSpec(
            num_scalar_prefetch=1,
            grid=(steps,),
            in_specs=[
                pl.BlockSpec((block, depth), lambda i, w: (w[0] * steps * skip + i, 0)),
                fixed(w.shape),
            ]
            + [part] * len(rows)
            + [fixed((1, model))] * len(vectors),
            out_specs=[part] * len(kinds) + [fixed((8, model))] * sums,
        ),
        out_shape=[jax.ShapeDtypeStruct((half, model), kind) for kind in kinds]
        + [jax.ShapeDtypeStruct((8, model), f32)] * sums,
        compiler_params=ROOMY,
        cost_estimate=INSTANT,
        name=name,
    )(where, x, w, *rows, *[vector.reshape(1, model) for vector in vectors])
    return list(results[: len(kinds)]) + [jnp.sum(value, axis=0) for value in results[len(kinds) :]]


def product_kernel(where, x, w, out):
    out[...] = mm(x[...], w[...], NT).astype(bf16)


def product_for_other(where, x, w, half, block=256):
    depth, model = x.shape[1], w.shape[0]
    steps = half // block
    skip = x.shape[0] > half
    return pl.pallas_call(
        product_kernel,
        grid_spec=pltpu.PrefetchScalarGridSpec(
            num_scalar_prefetch=1,
            grid=(steps,),
            in_specs=[
                pl.BlockSpec((block, depth), lambda i, w: ((1 - w[0]) * steps * skip + i, 0)),
                pl.BlockSpec(w.shape, lambda i, w: (0, 0)),
            ],
            out_specs=pl.BlockSpec((block, model), lambda i, w: (i, 0)),
        ),
        out_shape=jax.ShapeDtypeStruct((half, model), bf16),
        compiler_params=ROOMY,
        cost_estimate=INSTANT,
        name="product_for_other",
    )(where, x, w)


def finish_attention(value, away, tokens, bias, gain, shift):
    middle = tokens.astype(f32) + (value + away.astype(f32) + bias)
    unit, _ = norm_parts(middle)
    return (middle, unit * gain + shift), ()


def finish_output(value, away, middle, bias):
    return (middle + (value + away.astype(f32)) + bias,), ()


def norm_back(grad_out, values, gain):
    unit, inverse = norm_parts(values)
    scaled = grad_out * gain
    grad_in = inverse * (
        scaled
        - jnp.mean(scaled, axis=-1, keepdims=True)
        - unit * jnp.mean(scaled * unit, axis=-1, keepdims=True)
    )
    return grad_in, grad_out * unit


def finish_middle(value, away, middle, cotangent, gain):
    grad = value + away.astype(f32)
    back, by_gain = norm_back(grad, middle, gain)
    out_grad = cotangent.astype(f32)
    total = out_grad + back
    low = total.astype(bf16)
    return (total, low), (by_gain, grad, low.astype(f32), out_grad)


def finish_input(value, away, tokens, middle_grad, gain):
    grad = value + away.astype(f32)
    back, by_gain = norm_back(grad, tokens.astype(f32), gain)
    return (middle_grad + back,), (by_gain, grad)


def flip(size, bit):
    return [(i, i ^ bit) for i in range(size)]


def send(value, pairs, axis="dp"):
    return lax.ppermute(value, axis, pairs)


def tie(*values):
    leaves, tree = jax.tree.flatten(values)
    return jax.tree.unflatten(tree, lax.optimization_barrier(leaves))


def gather_slow(shard, size):
    ring = size // 4
    pieces = [shard] + [
        send(shard, [(i, (i + 4 * step) % size) for i in range(size)]) for step in range(1, ring)
    ]
    return jnp.stack(pieces)


def gather_near(own, size):
    return send(own, flip(size, 1)), send(own, flip(size, 2))


def gather_far(near, size):
    half = size // 8
    return send(near[0][:half], flip(size, 2)), send(near[1][half:], flip(size, 1))


def place_kernel(*refs, size, widths):
    index, pieces, outs, sem = refs[0][0], refs[1:6], refs[6:-1], refs[-1]
    high, low = index // 4, index % 4
    ring, rows = size // 4, pieces[0].shape[1]
    copies = []
    for piece, bits, first in zip(pieces, (0, 1, 2, 3, 3), (0, 0, 0, 0, ring // 2)):
        for step in range(piece.shape[0]):
            block = lax.rem(high - first - step + ring, ring) * 4 + (low ^ bits)
            to = pl.ds(pl.multiple_of(block * rows, rows), rows)
            start = 0
            for out, wide in zip(outs, widths):
                copies.append(
                    pltpu.make_async_copy(
                        piece.at[step, :, pl.ds(start, wide)], out.at[to, :], sem.at[len(copies)]
                    )
                )
                start += wide
    for copy in copies:
        copy.start()
    for copy in copies:
        copy.wait()


def place(own, near, far, size, widths):
    rows = own.shape[1]
    anywhere = pl.BlockSpec(memory_space=pl.ANY)
    return pl.pallas_call(
        functools.partial(place_kernel, size=size, widths=widths),
        in_specs=[pl.BlockSpec(memory_space=pltpu.SMEM)] + [anywhere] * 5,
        out_specs=[pl.BlockSpec(memory_space=pltpu.VMEM)] * len(widths),
        scratch_shapes=[pltpu.SemaphoreType.DMA((size * len(widths),))],
        out_shape=[jax.ShapeDtypeStruct((rows * size, wide), bf16) for wide in widths],
        compiler_params=pltpu.CompilerParams(vmem_limit_bytes=24 * 2**20),
        cost_estimate=INSTANT,
        name="place",
    )(lax.axis_index("dp").reshape(1), own, *near, *far)


def add_low(*parts):
    total = parts[0].astype(f32)
    for part in parts[1:]:
        total = total + part.astype(f32)
    return total.astype(bf16)


def scatter_order(ring):
    low, high = list(range(ring // 2)), list(range(ring // 2, ring))
    pick = lambda bits, steps: [(bits, step) for step in steps]
    return [
        pick(0, low + high),
        pick(1, high) + pick(3, high),
        pick(2, low) + pick(3, low),
        pick(1, low),
        pick(2, high),
    ]


def scatter_far(stacks, size):
    return send(stacks[1], flip(size, 1)), send(stacks[2], flip(size, 2))


def scatter_near(stacks, got, size):
    half = size // 8
    return (
        send(add_low(stacks[3], got[1][half:]), flip(size, 1)),
        send(add_low(stacks[4], got[0][half:]), flip(size, 2)),
    )


def scatter_slow(groups, size):
    ring = size // 4
    half = ring // 2
    low, high = [], []
    for stacks, got, more in groups:
        low.append(add_low(stacks[0][:half], more[0], got[1][:half]))
        high.append(add_low(stacks[0][half:], more[1], got[0][:half]))
    low, high = jnp.concatenate(low, axis=2), jnp.concatenate(high, axis=2)
    blocks = [low[step] for step in range(half)] + [high[step] for step in range(half)]
    return blocks[0], [
        send(blocks[step], [(i, (i + 4 * step) % size) for i in range(size)])
        for step in range(1, ring)
    ]


def scatter_last(own, got):
    return sum((part.astype(f32) for part in got), own.astype(f32))


def sum_everywhere(value, size):
    for bit in [1 << i for i in range(size.bit_length() - 1)]:
        value = value + send(value, flip(size, bit))
    return value + send(value, [(0, 1), (1, 0)], "tensor")


def on_device(
    size,
    tokens,
    cotangent,
    picture_ids,
    positions,
    valid,
    norm1_gain,
    norm1_bias,
    qkv_weight,
    qkv_bias,
    proj_weight,
    proj_bias,
    norm2_gain,
    norm2_bias,
    fc1_weight,
    fc1_bias,
    fc2_weight,
    fc2_bias,
):
    me = lax.axis_index("tensor")
    length = picture_ids.shape[0]
    half, model = tokens.shape
    rows = qkv_weight.shape[0]
    width = qkv_weight.shape[2]
    units = fc1_weight.shape[1]
    swap = [(0, 1), (1, 0)]
    cross = lambda value: send(value, swap, "tensor")

    gain_one, shift_one = norm1_gain.astype(f32), norm1_bias.astype(f32)
    gain_two, shift_two = norm2_gain.astype(f32), norm2_bias.astype(f32)
    qkv_shift = lax.dynamic_slice_in_dim(qkv_bias.astype(f32), me * width, width, 1).reshape(1, -1)
    fc1_shift = lax.dynamic_slice_in_dim(fc1_bias.astype(f32), me * units, units, 0).reshape(1, -1)

    where = jnp.stack([me, lax.axis_index("dp")]).astype(jnp.int32)
    inputs = tokens.astype(f32)
    unit_one, inverse_one = norm_parts(inputs)
    a_own = (unit_one * gain_one + shift_one).astype(bf16)
    a_other = cross(a_own)
    tables = rope_tables(positions, width)
    mq, mk = mask_lanes(picture_ids, valid, width // 128 - 1)

    qkv_own = gather_slow(qkv_weight.reshape(rows, 3 * width), size)
    joined = jnp.concatenate([proj_weight.T, fc1_weight], axis=1)
    cosine, down, up = tables
    qkv_own, joined, a_other, cosine, down = tie(qkv_own, joined, a_other, cosine, down)
    qkv_near = gather_near(qkv_own, size)
    own = gather_slow(joined, size)
    qkv_near, up, mq, mk = tie(qkv_near, up, mq, mk)
    qkv_far = gather_far(qkv_near, size)
    qkv_far, own = tie(qkv_far, own)
    tables = (cosine, down, up)
    near = gather_near(own, size)
    (qkv_full,) = place(qkv_own, qkv_near, qkv_far, size, [3 * width])
    q, k, v = qkv_rotate(where, a_own, a_other, qkv_full, qkv_shift, tables)
    pairs = mq.shape[0]
    mixed, lse_low = attend(mq, mk, q, k, v, 0, pairs // 2)
    near, mixed, fc2_shard = tie(near, mixed, fc2_weight.T)
    far = gather_far(near, size)
    fc2_turned = lax.all_gather(fc2_shard, "dp", axis=0, tiled=True)
    mixed, lse_high = attend(mq, mk, q, k, v, pairs // 2, pairs - pairs // 2, (mixed,))
    far, mixed = tie(far, mixed)
    proj_turned, fc1_full = place(own, near, far, size, [width, units])

    away = cross(product_for_other(where, mixed, proj_turned, half))
    middle, c_own = closing(
        where, mixed, proj_turned, [away, tokens], [proj_bias.astype(f32), gain_two, shift_two],
        finish_attention, [f32, bf16], 0, "middle",
    )
    grad_other = cross(cotangent)
    c_other = cross(c_own)
    hidden_own, slope_own = hidden_slope(c_own, fc1_full, fc1_shift)
    hidden_other, slope_other = hidden_slope(c_other, fc1_full, fc1_shift)

    fc2_stacks = weight_grad(where, [cotangent, grad_other], [hidden_own, hidden_other], size)
    fc2_turned, fc2_stacks = tie(fc2_turned, fc2_stacks)
    fc2_got = scatter_far(fc2_stacks, size)
    pre_other, bias_other = pre_grad(grad_other, fc2_turned, slope_other)
    part = product_for_other(where, pre_other, fc1_full, half)
    pre_own, bias_own = pre_grad(cotangent, fc2_turned, slope_own)
    fc2_got, pre_own, pre_other, part = tie(fc2_got, pre_own, pre_other, part)
    fc2_more = scatter_near(fc2_stacks, fc2_got, size)
    away = cross(part)
    fc1_stacks = weight_grad(where, [c_own, c_other], [pre_own, pre_other], size)
    fc2_more, fc1_stacks, pre_own, away, hidden_other = tie(
        fc2_more, fc1_stacks, pre_own, away, hidden_other
    )
    fc1_got = scatter_far(fc1_stacks, size)
    out_part = product_for_other(where, hidden_other, fc2_turned, half)
    (middle_grad, g_own, gain_two_grad, shift_two_grad, proj_shift_grad, fc2_shift_grad) = closing(
        where, pre_own, fc1_full, [away, middle, cotangent], [gain_two],
        finish_middle, [f32, bf16], 4, "middle_grad",
    )
    (output,) = closing(
        where, hidden_own, fc2_turned, [cross(out_part), middle], [fc2_bias.astype(f32)],
        finish_output, [f32], 0, "output",
    )
    fc1_got, g_own, output = tie(fc1_got, g_own, output)
    fc1_more = scatter_near(fc1_stacks, fc1_got, size)
    g_other = cross(g_own)
    mixed_grad = mixed_grad_rows(where, g_own, g_other, proj_turned)
    proj_grad = weight_grad(where, [g_own, g_other], [mixed])
    lse = jnp.concatenate([lse_low, lse_high], axis=0)
    fc1_more, mixed_grad, proj_grad = tie(fc1_more, mixed_grad, proj_grad)
    groups = [(fc2_stacks, fc2_got, fc2_more), (fc1_stacks, fc1_got, fc1_more)]
    kept, got = scatter_slow(groups, size)
    proj_shard = lax.psum_scatter(proj_grad, "dp", scatter_dimension=0, tiled=True)
    kept, mixed_grad = tie(kept, mixed_grad)
    qkv_grad = attend_back(mq, mk, q, k, v, mixed, mixed_grad, lse, tables)
    got, proj_shard, qkv_grad = tie(got, proj_shard, qkv_grad)
    qkv_stacks = weight_grad(where, [a_own, a_other], [qkv_grad], size)
    qkv_stacks, qkv_grad = tie(qkv_stacks, qkv_grad)
    qkv_got = scatter_far(qkv_stacks, size)
    part = product_for_other(where, qkv_grad, qkv_full, half)
    qkv_shift_grad = jnp.sum(qkv_grad.astype(f32), axis=0)
    input_grad, gain_one_grad, shift_one_grad = closing(
        where, qkv_grad, qkv_full, [cross(part), tokens, middle_grad], [gain_one],
        finish_input, [f32], 2, "input_grad",
    )
    qkv_got, input_grad, qkv_shift_grad, gain_one_grad = tie(
        qkv_got, input_grad, qkv_shift_grad, gain_one_grad
    )
    more = scatter_near(qkv_stacks, qkv_got, size)
    both_shards = scatter_last(kept, got)
    fc2_shard, fc1_shard = both_shards[:, :units], both_shards[:, units:]
    more, fc2_shard, fc1_shard = tie(more, fc2_shard, fc1_shard)
    kept, got = scatter_slow([(qkv_stacks, qkv_got, more)], size)
    qkv_shard = scatter_last(kept, got)

    fc1_shift_grad = jnp.sum(bias_own, axis=0) + jnp.sum(bias_other, axis=0)
    fc1_place = lax.dynamic_update_slice_in_dim(
        jnp.zeros((2 * units,), f32), fc1_shift_grad, me * units, 0
    )
    qkv_place = lax.dynamic_update_slice_in_dim(
        jnp.zeros((3, 2 * width), f32), qkv_shift_grad.reshape(3, width), me * width, 1
    )
    sums = [
        gain_one_grad, shift_one_grad, qkv_place.reshape(-1), proj_shift_grad,
        gain_two_grad, shift_two_grad, fc1_place, fc2_shift_grad,
    ]
    totals = sum_everywhere(jnp.concatenate(sums).reshape(-1, 128), size).reshape(-1)
    small = []
    for part in sums:
        small.append(totals[: part.shape[0]])
        totals = totals[part.shape[0] :]
    return (
        output,
        input_grad,
        small[0],
        small[1],
        qkv_shard.reshape(rows, 3, width),
        small[2].reshape(3, 2 * width),
        proj_shard.astype(f32).T,
        small[3],
        small[4],
        small[5],
        fc1_shard,
        small[6],
        fc2_shard.astype(f32).T,
        small[7],
    )


def norm_forward(values, gain, shift):
    center = values - jnp.mean(values, axis=-1, keepdims=True)
    inverse = lax.rsqrt(jnp.mean(center * center, axis=-1, keepdims=True) + EPS)
    unit = center * inverse
    return (unit * gain + shift, unit, inverse)


def on_any(
    tokens,
    cotangent,
    picture_ids,
    positions,
    valid,
    norm1_gain,
    norm1_bias,
    qkv_weight,
    qkv_bias,
    proj_weight,
    proj_bias,
    norm2_gain,
    norm2_bias,
    fc1_weight,
    fc1_bias,
    fc2_weight,
    fc2_bias,
):
    tensor_index = lax.axis_index("tensor")
    model_width = tokens.shape[1]
    local_width = qkv_weight.shape[2]
    local_hidden = fc1_weight.shape[1]
    local_heads = local_width // HEAD_DIM
    gain_one = norm1_gain.astype(jnp.float32)
    shift_one = norm1_bias.astype(jnp.float32)
    gain_two = norm2_gain.astype(jnp.float32)
    shift_two = norm2_bias.astype(jnp.float32)
    qkv_shift = lax.dynamic_slice_in_dim(
        qkv_bias.astype(jnp.float32), tensor_index * local_width, local_width, 1
    ).reshape(3 * local_width)
    fc1_shift = lax.dynamic_slice_in_dim(
        fc1_bias.astype(jnp.float32), tensor_index * local_hidden, local_hidden, 0
    )
    qkv_full, proj_full, fc1_full, fc2_full = (
        lax.all_gather(qkv_weight, "dp", axis=0, tiled=True),
        lax.all_gather(proj_weight, "dp", axis=1, tiled=True),
        lax.all_gather(fc1_weight, "dp", axis=0, tiled=True),
        lax.all_gather(fc2_weight, "dp", axis=1, tiled=True),
    )
    qkv_matrix = qkv_full.reshape(model_width, 3 * local_width)
    inputs = tokens.astype(jnp.float32)
    normed_one, unit_one, inverse_one = norm_forward(inputs, gain_one, shift_one)
    attn_in = lax.all_gather(normed_one.astype(jnp.bfloat16), "tensor", axis=0, tiled=True)
    total_rows = attn_in.shape[0]
    qkv_raw = jnp.dot(attn_in, qkv_matrix, preferred_element_type=jnp.float32) + qkv_shift
    pairs = -(-local_heads // 2)
    padded = 128 * (pairs + 1)
    fill = lambda value: jnp.pad(value, ((0, 0), (0, padded - local_width)))
    tables = [fill(table) for table in rope_tables(positions, local_width)]
    mq, mk = mask_lanes(picture_ids, valid, pairs)

    def rotate(part):
        turned = jnp.roll(part, -HEAD_DIM // 2, 1) * tables[1]
        return part * tables[0] + turned + jnp.roll(part, HEAD_DIM // 2, 1) * tables[2]

    split = [fill(part) for part in jnp.split(qkv_raw, 3, axis=1)]
    queries = (rotate(split[0]) * (HEAD_DIM**-0.5 * LOG2E)).astype(jnp.bfloat16)
    keys = rotate(split[1]).astype(jnp.bfloat16)
    values = split[2].astype(jnp.bfloat16)
    mixed_row, logsum_row = attend(mq, mk, queries, keys, values)
    attn_mixed = mixed_row[:, :local_width]
    piece = attn_mixed
    attn_out = lax.psum_scatter(
        jnp.dot(piece, proj_full, preferred_element_type=jnp.float32).astype(jnp.bfloat16),
        "tensor",
        scatter_dimension=0,
        tiled=True,
    ).astype(jnp.float32) + proj_bias.astype(jnp.float32)
    middle = inputs + attn_out
    normed_two, unit_two, inverse_two = norm_forward(middle, gain_two, shift_two)
    mlp_in = lax.all_gather(normed_two.astype(jnp.bfloat16), "tensor", axis=0, tiled=True)
    hidden_pre = jnp.dot(mlp_in, fc1_full, preferred_element_type=jnp.float32) + fc1_shift
    sigmoid_gate = jax.nn.sigmoid(1.702 * hidden_pre)
    hidden = (hidden_pre * sigmoid_gate).astype(jnp.bfloat16)
    piece = hidden
    mlp_out = lax.psum_scatter(
        jnp.dot(piece, fc2_full, preferred_element_type=jnp.float32).astype(jnp.bfloat16),
        "tensor",
        scatter_dimension=0,
        tiled=True,
    ).astype(jnp.float32) + fc2_bias.astype(jnp.float32)
    output = middle + mlp_out
    qkv_back, proj_back, fc1_back, fc2_back = (
        lax.all_gather(qkv_weight, "dp", axis=0, tiled=True),
        lax.all_gather(proj_weight, "dp", axis=1, tiled=True),
        lax.all_gather(fc1_weight, "dp", axis=0, tiled=True),
        lax.all_gather(fc2_weight, "dp", axis=1, tiled=True),
    )
    qkv_back = qkv_back.reshape(model_width, 3 * local_width)
    out_grad = cotangent.astype(jnp.float32)
    fc2_shift_grad = jnp.sum(out_grad, axis=0)
    out_grad_full = lax.all_gather(cotangent, "tensor", axis=0, tiled=True)
    fc2_grad = jnp.dot(hidden.T, out_grad_full, preferred_element_type=jnp.float32)
    hidden_grad = jnp.dot(out_grad_full, fc2_back.T, preferred_element_type=jnp.float32)
    slope = sigmoid_gate + 1.702 * hidden_pre * sigmoid_gate * (1.0 - sigmoid_gate)
    pre_grad = (hidden_grad * slope).astype(jnp.bfloat16)
    fc1_shift_grad = jnp.sum(pre_grad.astype(jnp.float32), axis=0)
    fc1_grad = jnp.dot(mlp_in.T, pre_grad, preferred_element_type=jnp.float32)
    piece = pre_grad
    normed_two_grad = lax.psum_scatter(
        jnp.dot(piece, fc1_back.T, preferred_element_type=jnp.float32).astype(jnp.bfloat16),
        "tensor",
        scatter_dimension=0,
        tiled=True,
    ).astype(jnp.float32)
    middle_part, gain_two_grad, shift_two_grad = norm_backward(
        normed_two_grad, unit_two, inverse_two, gain_two
    )
    middle_grad = out_grad + middle_part
    attn_grad_low = middle_grad.astype(jnp.bfloat16)
    proj_shift_grad = jnp.sum(attn_grad_low.astype(jnp.float32), axis=0)
    attn_grad_full = lax.all_gather(attn_grad_low, "tensor", axis=0, tiled=True)
    proj_grad = jnp.dot(attn_mixed.T, attn_grad_full, preferred_element_type=jnp.float32)
    mixed_grad = jnp.dot(attn_grad_full, proj_back.T, preferred_element_type=jnp.float32).astype(
        jnp.bfloat16
    )
    qkv_grad = attend_back(
        mq, mk, queries, keys, values, mixed_row, fill(mixed_grad), logsum_row, tables
    )
    qkv_grad = jnp.concatenate(
        [qkv_grad[:, at : at + local_width] for at in (0, padded, 2 * padded)], axis=1
    )
    qkv_shift_grad = jnp.sum(qkv_grad.astype(jnp.float32), axis=0)
    qkv_grad_weight = jnp.dot(attn_in.T, qkv_grad, preferred_element_type=jnp.float32)
    qkv_grad_weight = qkv_grad_weight.reshape(model_width, 3, local_width)
    piece = qkv_grad
    normed_one_grad = lax.psum_scatter(
        jnp.dot(piece, qkv_back.T, preferred_element_type=jnp.float32).astype(jnp.bfloat16),
        "tensor",
        scatter_dimension=0,
        tiled=True,
    ).astype(jnp.float32)
    input_part, gain_one_grad, shift_one_grad = norm_backward(
        normed_one_grad, unit_one, inverse_one, gain_one
    )
    input_grad = middle_grad + input_part
    qkv_grad_shard, proj_grad_shard, fc1_grad_shard, fc2_grad_shard = (
        lax.psum_scatter(
            qkv_grad_weight.astype(jnp.bfloat16), "dp", scatter_dimension=0, tiled=True
        ).astype(jnp.float32),
        lax.psum_scatter(
            proj_grad.astype(jnp.bfloat16), "dp", scatter_dimension=1, tiled=True
        ).astype(jnp.float32),
        lax.psum_scatter(
            fc1_grad.astype(jnp.bfloat16), "dp", scatter_dimension=0, tiled=True
        ).astype(jnp.float32),
        lax.psum_scatter(
            fc2_grad.astype(jnp.bfloat16), "dp", scatter_dimension=1, tiled=True
        ).astype(jnp.float32),
    )
    qkv_shift_full = lax.dynamic_update_slice_in_dim(
        jnp.zeros((3, model_width), jnp.float32),
        qkv_shift_grad.reshape(3, local_width),
        tensor_index * local_width,
        1,
    )
    fc1_shift_full = lax.dynamic_update_slice_in_dim(
        jnp.zeros((fc1_bias.shape[0],), jnp.float32), fc1_shift_grad, tensor_index * local_hidden, 0
    )
    summed = lax.psum(
        (
            gain_one_grad,
            shift_one_grad,
            qkv_shift_full,
            proj_shift_grad,
            gain_two_grad,
            shift_two_grad,
            fc1_shift_full,
            fc2_shift_grad,
        ),
        ("dp", "tensor"),
    )
    return (
        output,
        input_grad,
        summed[0],
        summed[1],
        qkv_grad_shard,
        summed[2],
        proj_grad_shard,
        summed[3],
        summed[4],
        summed[5],
        fc1_grad_shard,
        summed[6],
        fc2_grad_shard,
        summed[7],
    )


def solution(mesh):
    size = mesh.shape["dp"]
    paired = mesh.shape["tensor"] == 2 and size == 16
    return jax.shard_map(
        functools.partial(on_device, size) if paired else on_any,
        mesh=mesh,
        in_specs=(
            P(("dp", "tensor"), None),
            P(("dp", "tensor"), None),
            P("dp"),
            P(None, "dp"),
            P("dp"),
            P(),
            P(),
            P("dp", None, "tensor"),
            P(),
            P("tensor", "dp"),
            P(),
            P(),
            P(),
            P("dp", "tensor"),
            P(),
            P("tensor", "dp"),
            P(),
        ),
        out_specs=(
            P(("dp", "tensor"), None),
            P(("dp", "tensor"), None),
            P(),
            P(),
            P("dp", None, "tensor"),
            P(),
            P("tensor", "dp"),
            P(),
            P(),
            P(),
            P("dp", "tensor"),
            P(),
            P("tensor", "dp"),
            P(),
        ),
        check_vma=False,
    )
```

```python
import functools
import math

import jax
import jax.numpy as jnp
from jax import lax
from jax.experimental import pallas as pl
from jax.experimental.pallas import tpu as pltpu
from jax.sharding import PartitionSpec as P

HEAD_DIM = 80
EPS = 1e-06
LOG2E = math.log2(math.e)
FAR = 1e30
f32 = jnp.float32
bf16 = jnp.bfloat16
NT = (((1,), (1,)), ((), ()))
NN = (((1,), (0,)), ((), ()))
TN = (((0,), (0,)), ((), ()))


INSTANT = pl.CostEstimate(flops=1, bytes_accessed=1, transcendentals=0)
ROOMY = pltpu.CompilerParams(vmem_limit_bytes=62 * 2**20)
MODEST = pltpu.CompilerParams(vmem_limit_bytes=32 * 2**20)


def mm(left, right, dims):
    return lax.dot_general(left, right, dims, preferred_element_type=f32)


def whole(shape):
    return pl.BlockSpec(shape, lambda i: (0,) * len(shape))


def norm_parts(values):
    center = values - jnp.mean(values, axis=-1, keepdims=True)
    inverse = lax.rsqrt(jnp.mean(center * center, axis=-1, keepdims=True) + EPS)
    return center * inverse, inverse


def norm_backward(grad_out, unit, inverse, gain):
    scaled = grad_out * gain
    grad_in = inverse * (
        scaled
        - jnp.mean(scaled, axis=-1, keepdims=True)
        - unit * jnp.mean(scaled * unit, axis=-1, keepdims=True)
    )
    return (grad_in, jnp.sum(grad_out * unit, axis=0), jnp.sum(grad_out, axis=0))


def rope_tables(place, width):
    quarter = HEAD_DIM // 4
    freqs = 10000.0 ** (-2.0 * jnp.arange(quarter, dtype=f32) / (HEAD_DIM // 2))
    along_rows = place[0].astype(f32)[:, None] * freqs[None, :]
    along_cols = place[1].astype(f32)[:, None] * freqs[None, :]
    theta = jnp.concatenate([along_rows, along_cols], axis=1)
    lane = jnp.arange(width)[None, :] % HEAD_DIM
    entry = jnp.arange(HEAD_DIM // 2)[:, None]
    low = jnp.where(lane == entry, 1.0, 0.0)
    high = jnp.where(lane == entry + HEAD_DIM // 2, 1.0, 0.0)
    exact = functools.partial(jnp.dot, precision=lax.Precision.HIGHEST)
    cosine, sine = jnp.cos(theta), jnp.sin(theta)
    return exact(cosine, low + high), exact(sine, -low), exact(sine, high)


def mask_lanes(picture, valid, pairs):
    lane = jnp.arange(256)[None, None, :]
    pair = jnp.arange(pairs)[:, None, None]
    spare = (lane - 32 * pair - 160) % 256
    ident = picture[None, :, None]
    dead = (valid <= 0).astype(f32)[None, :, None]
    for_query = jnp.where(
        spare < 4, jnp.where(spare == ident, 0.0, -FAR), jnp.where(spare == 4, -FAR, 0.0)
    )
    for_key = jnp.where(
        spare < 4, jnp.where(spare == ident, 1.0, 0.0), jnp.where(spare == 4, dead, 0.0)
    )
    return for_query.astype(bf16), for_key.astype(bf16)


def window_lanes(pair):
    place = lax.broadcasted_iota(jnp.int32, (1, 256), 1) - 32 * pair
    first = (place >= 0) & (place < HEAD_DIM)
    second = (place >= HEAD_DIM) & (place < 2 * HEAD_DIM)
    return first, second, (place - 2 * HEAD_DIM) & 255


def as_ones(condition):
    return jnp.where(condition, 1.0, 0.0).astype(bf16)


def reach(length, block):
    half, most = length // 2, 3 * length // 4
    spans = []
    for start in range(0, length, block):
        if start + block <= half:
            spans.append((start, 0, most))
        elif start >= most:
            spans.append((start, half, length))
        else:
            spans.append((start, 0, length))
    return spans


def attend_kernel(*refs, block, begin):
    mq_ref, mk_ref, q_ref, k_ref, v_ref = refs[:5]
    o_ref, lse_ref, qs, ks, vs = refs[-5:]
    length = q_ref.shape[0]
    pair = pl.program_id(0) + begin
    if begin:

        @pl.when(pl.program_id(0) == 0)
        def _():
            o_ref[...] = refs[5][...]

    win = pl.ds(pl.multiple_of(128 * pair, 128), 256)
    first, second, spare = window_lanes(pair)
    both = first | second
    m0, m1, mp = as_ones(first), as_ones(second), as_ones(both)
    count0, count1 = as_ones(spare == 5), as_ones(spare == 6)
    for start in range(0, length, 512):
        rows = pl.ds(start, 512)
        mk = mk_ref[0, rows, :]
        k, v = k_ref[rows, win], v_ref[rows, win]
        qs[rows, :] = q_ref[rows, win] * mp + mq_ref[0, rows, :]
        ks[0, rows, :] = k * m0 + mk
        ks[1, rows, :] = k * m1 + mk
        vs[0, rows, :] = v * m0 + count0
        vs[1, rows, :] = v * m1 + count1
    for start, low, high in reach(length, block):
        rows, keys = pl.ds(start, block), pl.ds(low, high - low)
        weights, peaks = [], []
        for head in range(2):
            scores = mm(qs[rows, :], ks[head, keys, :], NT)
            peak = jnp.max(scores, axis=1, keepdims=True)
            peaks.append(peak)
            weights.append(jnp.exp2(scores - peak).astype(bf16))
        mixed = mm(
            jnp.concatenate(weights, 1),
            jnp.concatenate([vs[0, keys, :], vs[1, keys, :]], 0),
            NN,
        )
        total0 = jnp.sum(jnp.where(spare == 5, mixed, 0.0), axis=1, keepdims=True)
        total1 = jnp.sum(jnp.where(spare == 6, mixed, 0.0), axis=1, keepdims=True)
        mixed = mixed * jnp.where(first, 1.0 / total0, 1.0 / total1)
        o_ref[rows, win] = jnp.where(both, mixed, o_ref[rows, win].astype(f32)).astype(bf16)
        lane = lax.broadcasted_iota(jnp.int32, (block, 128), 1)
        sums = jnp.where(
            lane == 0,
            peaks[0] + jnp.log2(total0),
            jnp.where(lane == 1, peaks[1] + jnp.log2(total1), 0.0),
        )
        lse_ref[0, :, rows] = jnp.transpose(sums)[:8, :]


def attend(mq, mk, q, k, v, begin=0, count=None, before=(), block=512):
    length, width = q.shape
    count = mq.shape[0] - begin if count is None else count
    part = lambda shape, skip: pl.BlockSpec(shape, lambda i: (i + skip, 0, 0))
    return pl.pallas_call(
        functools.partial(attend_kernel, block=block, begin=begin),
        grid=(count,),
        in_specs=[part((1, length, 256), begin)] * 2
        + [whole((length, width))] * (3 + len(before)),
        out_specs=[whole((length, width)), part((1, 8, length), 0)],
        scratch_shapes=[pltpu.VMEM((length, 256), bf16)]
        + [pltpu.VMEM((2, length, 256), bf16)] * 2,
        out_shape=[
            jax.ShapeDtypeStruct((length, width), bf16),
            jax.ShapeDtypeStruct((count, 8, length), f32),
        ],
        compiler_params=ROOMY,
        cost_estimate=INSTANT,
        name="attend",
    )(mq, mk, q, k, v, *before)


def attend_back_kernel(
    mq_ref, mk_ref, q_ref, k_ref, v_ref, o_ref, g_ref, lse_ref, cos_ref, down_ref, up_ref,
    out_ref, qs, ks, gs, dq, center, *, block, step,
):
    length, width = q_ref.shape
    pair = pl.program_id(0)
    win = pl.ds(pl.multiple_of(128 * pair, 128), 256)
    first, second, _ = window_lanes(pair)
    both = first | second
    m0, m1 = as_ones(first), as_ones(second)
    row = lax.broadcasted_iota(jnp.int32, (8, 256), 0)
    pick = as_ones(((row == 0) & first) | ((row == 1) & second))
    for start in range(0, length, 512):
        rows = pl.ds(start, 512)
        mq, mk = mq_ref[0, rows, :], mk_ref[0, rows, :]
        q, k, g = q_ref[rows, win], k_ref[rows, win], g_ref[rows, win]
        qs[0, rows, :] = q * m0 + mq
        qs[1, rows, :] = q * m1 + mq
        ks[0, rows, :] = k * m0 + mk
        ks[1, rows, :] = k * m1 + mk
        gs[0, rows, :] = g * m0
        gs[1, rows, :] = g * m1
        product = g.astype(f32) * o_ref[rows, win].astype(f32)
        high = product.astype(bf16)
        low = (product - high.astype(f32)).astype(bf16)
        center[:, rows] = mm(pick, high, NT) + mm(pick, low, NT)
        dq[rows, :] = jnp.zeros((512, 256), f32)

    def turn_back(grad, rows):
        turned = (
            pltpu.roll(grad, 256 - HEAD_DIM // 2, 1) * down_ref[rows, win]
            + pltpu.roll(grad, HEAD_DIM // 2, 1) * up_ref[rows, win]
        )
        return grad * cos_ref[rows, win] - turned

    def put(grad, rows, part):
        to = pl.ds(pl.multiple_of(128 * pair + part * width, 128), 256)
        out_ref[rows, to] = jnp.where(both, grad, out_ref[rows, to].astype(f32)).astype(bf16)

    for start, low, high in reach(length, block):
        keys = pl.ds(start, block)
        v = v_ref[keys, win]
        dk = dv = None
        for at in range(low, high, step):
            rows = pl.ds(at, min(step, high - at))
            probs, grads = [], []
            for head in range(2):
                scores = mm(ks[head, keys, :], qs[head, rows, :], NT)
                prob_grad = mm(v, gs[head, rows, :], NT)
                prob = jnp.exp2(scores - lse_ref[0, head : head + 1, rows])
                probs.append(prob.astype(bf16))
                grads.append((prob * (prob_grad - center[head : head + 1, rows])).astype(bf16))
            dv_part = mm(
                jnp.concatenate(probs, 1),
                jnp.concatenate([gs[0, rows, :], gs[1, rows, :]], 0),
                NN,
            )
            dk_part = mm(
                jnp.concatenate(grads, 1),
                jnp.concatenate([qs[0, rows, :], qs[1, rows, :]], 0),
                NN,
            )
            dv = dv_part if dv is None else dv + dv_part
            dk = dk_part if dk is None else dk + dk_part
            dq[rows, :] += mm(
                jnp.concatenate(grads, 0),
                jnp.concatenate([ks[0, keys, :], ks[1, keys, :]], 0),
                TN,
            )
        put(turn_back(dk * (1.0 / LOG2E), keys), keys, 1)
        put(dv, keys, 2)
    for start in range(0, length, 512):
        rows = pl.ds(start, 512)
        put(turn_back(dq[rows, :] * HEAD_DIM**-0.5, rows), rows, 0)


def attend_back(mq, mk, q, k, v, o, g, lse, tables, block=512, step=1024):
    length, width = q.shape
    pairs = width // 128 - 1
    part = lambda shape: pl.BlockSpec(shape, lambda i: (i, 0, 0))
    return pl.pallas_call(
        functools.partial(attend_back_kernel, block=block, step=step),
        grid=(pairs,),
        in_specs=[part((1, length, 256))] * 2
        + [whole((length, width))] * 5
        + [part((1, 8, length))]
        + [whole((length, width))] * 3,
        out_specs=whole((length, 3 * width)),
        scratch_shapes=[pltpu.VMEM((2, length, 256), bf16)] * 3
        + [pltpu.VMEM((length, 256), f32), pltpu.VMEM((8, length), f32)],
        out_shape=jax.ShapeDtypeStruct((length, 3 * width), bf16),
        compiler_params=pltpu.CompilerParams(vmem_limit_bytes=63 * 2**20),
        cost_estimate=INSTANT,
        name="attend_back",
    )(mq, mk, q, k, v, o, g, lse, *tables)


def qkv_kernel(where, own, other, w, b, cos, down, up, q, k, v):
    width = q.shape[1]
    mine = pl.program_id(0) // (pl.num_programs(0) // 2) == where[0]
    x = mm(jnp.where(mine, own[...], other[...]), w[...], NN) + b[...]

    def rotate(part):
        return (
            part * cos[...]
            + pltpu.roll(part, width - HEAD_DIM // 2, 1) * down[...]
            + pltpu.roll(part, HEAD_DIM // 2, 1) * up[...]
        )

    q[...] = (rotate(x[:, :width]) * (HEAD_DIM**-0.5 * LOG2E)).astype(bf16)
    k[...] = rotate(x[:, width : 2 * width]).astype(bf16)
    v[...] = x[:, 2 * width :].astype(bf16)


def qkv_rotate(where, own, other, w, b, tables, block=512):
    half, depth = own.shape
    width = w.shape[1] // 3
    steps = half // block
    rows = lambda n: pl.BlockSpec((block, n), lambda i, w: (i, 0))
    part = pl.BlockSpec((block, depth), lambda i, w: (i % steps, 0))
    fixed = lambda shape: pl.BlockSpec(shape, lambda i, w: (0, 0))
    return pl.pallas_call(
        qkv_kernel,
        grid_spec=pltpu.PrefetchScalarGridSpec(
            num_scalar_prefetch=1,
            grid=(2 * steps,),
            in_specs=[part, part, fixed(w.shape), fixed(b.shape)] + [rows(width)] * 3,
            out_specs=[rows(width)] * 3,
        ),
        out_shape=[jax.ShapeDtypeStruct((2 * half, width), bf16)] * 3,
        compiler_params=ROOMY,
        cost_estimate=INSTANT,
        name="qkv_rotate",
    )(where, own, other, w, b, *tables)


def hidden_kernel(c, w, b, hidden, slope):
    pre = mm(c[...], w[...], NN) + b[...]
    gate = 1.0 / (1.0 + jnp.exp2(pre * (-1.702 * LOG2E)))
    value = pre * gate
    hidden[...] = value.astype(bf16)
    slope[...] = (gate + 1.702 * value * (1.0 - gate)).astype(bf16)


def hidden_slope(c, w, b, block=128):
    length, depth = c.shape
    units = w.shape[1]
    rows = lambda n: pl.BlockSpec((block, n), lambda i: (i, 0))
    return pl.pallas_call(
        hidden_kernel,
        grid=(length // block,),
        in_specs=[rows(depth), whole(w.shape), whole(b.shape)],
        out_specs=[rows(units)] * 2,
        out_shape=[jax.ShapeDtypeStruct((length, units), bf16)] * 2,
        compiler_params=ROOMY,
        cost_estimate=INSTANT,
        name="hidden_slope",
    )(c, w, b)


def pre_grad_kernel(g, w, slope, out, bias):
    grad = (mm(g[...], w[...], NN) * slope[...].astype(f32)).astype(bf16)
    out[...] = grad

    @pl.when(pl.program_id(0) == 0)
    def _():
        bias[...] = jnp.zeros(bias.shape, f32)

    bias[...] += jnp.sum(grad.astype(f32).reshape(-1, 8, grad.shape[1]), axis=0)


def pre_grad(g, w, slope, block=256):
    length, depth = g.shape
    units = w.shape[1]
    rows = lambda n: pl.BlockSpec((block, n), lambda i: (i, 0))
    return pl.pallas_call(
        pre_grad_kernel,
        grid=(length // block,),
        in_specs=[rows(depth), whole(w.shape), rows(units)],
        out_specs=[rows(units), whole((8, units))],
        out_shape=[
            jax.ShapeDtypeStruct((length, units), bf16),
            jax.ShapeDtypeStruct((8, units), f32),
        ],
        compiler_params=ROOMY,
        cost_estimate=INSTANT,
        name="pre_grad",
    )(g, w, slope)


def weight_grad_kernel(*refs, count, size):
    where = refs[0]
    lefts, rights = refs[1 : 1 + count], refs[1 + count : 1 + 2 * count]
    outs = refs[1 + 2 * count :]
    total = None
    for left, right in zip(lefts, rights):
        part = mm(left[...], right[...], TN)
        total = part if total is None else total + part
    if not size:
        outs[0][...] = total.astype(bf16)
        return
    result = outs[-1]
    result[...] = total.astype(bf16)
    index = where[1]
    high, low = index // 4, index % 4
    ring, rows = size // 4, outs[0].shape[1]
    for out, order in zip(outs, scatter_order(ring)):
        for slot, (bits, step) in enumerate(order):
            block = lax.rem(high + step, ring) * 4 + (low ^ bits)
            out[slot] = result[pl.ds(pl.multiple_of(block * rows, rows), rows), :]


def weight_grad(where, lefts, rights, size=0, block=512):
    length, high = lefts[0].shape
    wide = rights[0].shape[1]
    if len(rights) == 1:
        rights = rights * 2
        specs = [
            pl.BlockSpec((length, block), lambda i, w: (w[0], i)),
            pl.BlockSpec((length, block), lambda i, w: (1 - w[0], i)),
        ]
    else:
        specs = [pl.BlockSpec((length, block), lambda i, w: (0, i))] * 2
    if size:
        stacks = [(len(order), high // size) for order in scatter_order(size // 4)]
        out_specs = [pl.BlockSpec(stack + (block,), lambda i, w: (0, 0, i)) for stack in stacks]
        out_shape = [jax.ShapeDtypeStruct(stack + (wide,), bf16) for stack in stacks]
        scratch = [pltpu.VMEM((high, block), bf16)]
    else:
        out_specs = pl.BlockSpec((high, block), lambda i, w: (0, i))
        out_shape = jax.ShapeDtypeStruct((high, wide), bf16)
        scratch = []
    return pl.pallas_call(
        functools.partial(weight_grad_kernel, count=2, size=size),
        grid_spec=pltpu.PrefetchScalarGridSpec(
            num_scalar_prefetch=1,
            grid=(pl.cdiv(wide, block),),
            in_specs=[pl.BlockSpec((length, high), lambda i, w: (0, 0))] * 2 + specs,
            out_specs=out_specs,
            scratch_shapes=scratch,
        ),
        out_shape=out_shape,
        compiler_params=MODEST if wide < high else ROOMY,
        cost_estimate=INSTANT,
        name="weight_grad",
    )(where, *lefts, *rights)


def mixed_grad_kernel(where, own, other, w, out):
    value = jnp.where(pl.program_id(0) < pl.num_programs(0) // 2, own[...], other[...])
    out[...] = mm(value, w[...], NN).astype(bf16)


def mixed_grad_rows(where, own, other, w, block=512):
    half, depth = own.shape
    wide = w.shape[1]
    steps = half // block
    return pl.pallas_call(
        mixed_grad_kernel,
        grid_spec=pltpu.PrefetchScalarGridSpec(
            num_scalar_prefetch=1,
            grid=(2 * steps,),
            in_specs=[
                pl.BlockSpec((block, depth), lambda i, w: (jnp.minimum(i, steps - 1), 0)),
                pl.BlockSpec((block, depth), lambda i, w: (jnp.maximum(i - steps, 0), 0)),
                pl.BlockSpec((depth, wide), lambda i, w: (0, 0)),
            ],
            out_specs=pl.BlockSpec(
                (block, wide), lambda i, w: ((w[0] * steps + i) % (2 * steps), 0)
            ),
        ),
        out_shape=jax.ShapeDtypeStruct((2 * half, wide), bf16),
        compiler_params=MODEST,
        cost_estimate=INSTANT,
        name="mixed_grad",
    )(where, own, other, w)


def closing_kernel(*refs, finish, extras, outs):
    x, w = refs[1:3]
    given = [ref[...] for ref in refs[3 : 3 + extras]]
    results, sums = finish(mm(x[...], w[...], NT), *given)
    for ref, value in zip(refs[3 + extras : 3 + extras + outs], results):
        ref[...] = value.astype(ref.dtype)
    totals = refs[3 + extras + outs :]

    @pl.when(pl.program_id(0) == 0)
    def _():
        for ref in totals:
            ref[...] = jnp.zeros(ref.shape, f32)

    for ref, value in zip(totals, sums):
        ref[...] += jnp.sum(value.reshape(-1, 8, value.shape[1]), axis=0)


def closing(where, x, w, rows, vectors, finish, kinds, sums, name, block=256):
    half, model = rows[0].shape
    depth = x.shape[1]
    steps = half // block
    skip = x.shape[0] > half
    part = pl.BlockSpec((block, model), lambda i, w: (i, 0))
    fixed = lambda shape: pl.BlockSpec(shape, lambda i, w: (0, 0))
    results = pl.pallas_call(
        functools.partial(
            closing_kernel, finish=finish, extras=len(rows) + len(vectors), outs=len(kinds)
        ),
        grid_spec=pltpu.PrefetchScalarGridSpec(
            num_scalar_prefetch=1,
            grid=(steps,),
            in_specs=[
                pl.BlockSpec((block, depth), lambda i, w: (w[0] * steps * skip + i, 0)),
                fixed(w.shape),
            ]
            + [part] * len(rows)
            + [fixed((1, model))] * len(vectors),
            out_specs=[part] * len(kinds) + [fixed((8, model))] * sums,
        ),
        out_shape=[jax.ShapeDtypeStruct((half, model), kind) for kind in kinds]
        + [jax.ShapeDtypeStruct((8, model), f32)] * sums,
        compiler_params=MODEST if depth < model else ROOMY,
        cost_estimate=INSTANT,
        name=name,
    )(where, x, w, *rows, *[vector.reshape(1, model) for vector in vectors])
    return list(results[: len(kinds)]) + [jnp.sum(value, axis=0) for value in results[len(kinds) :]]


def product_kernel(where, x, w, out):
    out[...] = mm(x[...], w[...], NT).astype(bf16)


def product_for_other(where, x, w, half, block=256):
    depth, model = x.shape[1], w.shape[0]
    steps = half // block
    skip = x.shape[0] > half
    return pl.pallas_call(
        product_kernel,
        grid_spec=pltpu.PrefetchScalarGridSpec(
            num_scalar_prefetch=1,
            grid=(steps,),
            in_specs=[
                pl.BlockSpec((block, depth), lambda i, w: ((1 - w[0]) * steps * skip + i, 0)),
                pl.BlockSpec(w.shape, lambda i, w: (0, 0)),
            ],
            out_specs=pl.BlockSpec((block, model), lambda i, w: (i, 0)),
        ),
        out_shape=jax.ShapeDtypeStruct((half, model), bf16),
        compiler_params=MODEST if depth < w.shape[0] else ROOMY,
        cost_estimate=INSTANT,
        name="product_for_other",
    )(where, x, w)


def finish_attention(value, away, tokens, bias, gain, shift):
    middle = tokens.astype(f32) + (value + away.astype(f32) + bias)
    unit, _ = norm_parts(middle)
    return (middle, unit * gain + shift), ()


def finish_output(value, away, middle, bias):
    return (middle + (value + away.astype(f32)) + bias,), ()


def norm_back(grad_out, values, gain):
    unit, inverse = norm_parts(values)
    scaled = grad_out * gain
    grad_in = inverse * (
        scaled
        - jnp.mean(scaled, axis=-1, keepdims=True)
        - unit * jnp.mean(scaled * unit, axis=-1, keepdims=True)
    )
    return grad_in, grad_out * unit


def finish_middle(value, away, middle, cotangent, gain):
    grad = value + away.astype(f32)
    back, by_gain = norm_back(grad, middle, gain)
    out_grad = cotangent.astype(f32)
    total = out_grad + back
    low = total.astype(bf16)
    return (total, low), (by_gain, grad, low.astype(f32), out_grad)


def finish_input(value, away, tokens, middle_grad, gain):
    grad = value + away.astype(f32)
    back, by_gain = norm_back(grad, tokens.astype(f32), gain)
    return (middle_grad + back,), (by_gain, grad)


def flip(size, bit):
    return [(i, i ^ bit) for i in range(size)]


def send(value, pairs, axis="dp"):
    return lax.ppermute(value, axis, pairs)


def tie(*values):
    leaves, tree = jax.tree.flatten(values)
    return jax.tree.unflatten(tree, lax.optimization_barrier(leaves))


def gather_slow(shard, size):
    ring = size // 4
    pieces = [shard] + [
        send(shard, [(i, (i + 4 * step) % size) for i in range(size)]) for step in range(1, ring)
    ]
    return jnp.stack(pieces)


def gather_near(own, size):
    return send(own, flip(size, 1)), send(own, flip(size, 2))


def gather_far(near, size):
    half = size // 8
    return send(near[0][:half], flip(size, 2)), send(near[1][half:], flip(size, 1))


def place_kernel(*refs, size, widths):
    index, pieces, outs, sem = refs[0][0], refs[1:6], refs[6:-1], refs[-1]
    high, low = index // 4, index % 4
    ring, rows = size // 4, pieces[0].shape[1]
    copies = []
    for piece, bits, first in zip(pieces, (0, 1, 2, 3, 3), (0, 0, 0, 0, ring // 2)):
        for step in range(piece.shape[0]):
            block = lax.rem(high - first - step + ring, ring) * 4 + (low ^ bits)
            to = pl.ds(pl.multiple_of(block * rows, rows), rows)
            start = 0
            for out, wide in zip(outs, widths):
                copies.append(
                    pltpu.make_async_copy(
                        piece.at[step, :, pl.ds(start, wide)], out.at[to, :], sem.at[len(copies)]
                    )
                )
                start += wide
    for copy in copies:
        copy.start()
    for copy in copies:
        copy.wait()


def place(own, near, far, size, widths):
    rows = own.shape[1]
    anywhere = pl.BlockSpec(memory_space=pl.ANY)
    return pl.pallas_call(
        functools.partial(place_kernel, size=size, widths=widths),
        in_specs=[pl.BlockSpec(memory_space=pltpu.SMEM)] + [anywhere] * 5,
        out_specs=[pl.BlockSpec(memory_space=pltpu.VMEM)] * len(widths),
        scratch_shapes=[pltpu.SemaphoreType.DMA((size * len(widths),))],
        out_shape=[jax.ShapeDtypeStruct((rows * size, wide), bf16) for wide in widths],
        compiler_params=pltpu.CompilerParams(vmem_limit_bytes=24 * 2**20),
        cost_estimate=INSTANT,
        name="place",
    )(lax.axis_index("dp").reshape(1), own, *near, *far)


def add_low(*parts):
    total = parts[0].astype(f32)
    for part in parts[1:]:
        total = total + part.astype(f32)
    return total.astype(bf16)


def scatter_order(ring):
    low, high = list(range(ring // 2)), list(range(ring // 2, ring))
    pick = lambda bits, steps: [(bits, step) for step in steps]
    return [
        pick(0, low + high),
        pick(1, high) + pick(3, high),
        pick(2, low) + pick(3, low),
        pick(1, low),
        pick(2, high),
    ]


def scatter_far(stacks, size):
    return send(stacks[1], flip(size, 1)), send(stacks[2], flip(size, 2))


def scatter_near(stacks, got, size):
    half = size // 8
    return (
        send(add_low(stacks[3], got[1][half:]), flip(size, 1)),
        send(add_low(stacks[4], got[0][half:]), flip(size, 2)),
    )


def scatter_slow(groups, size):
    ring = size // 4
    half = ring // 2
    low, high = [], []
    for stacks, got, more in groups:
        low.append(add_low(stacks[0][:half], more[0], got[1][:half]))
        high.append(add_low(stacks[0][half:], more[1], got[0][:half]))
    low, high = jnp.concatenate(low, axis=2), jnp.concatenate(high, axis=2)
    blocks = [low[step] for step in range(half)] + [high[step] for step in range(half)]
    return blocks[0], [
        send(blocks[step], [(i, (i + 4 * step) % size) for i in range(size)])
        for step in range(1, ring)
    ]


def scatter_last(own, got):
    return sum((part.astype(f32) for part in got), own.astype(f32))


def sum_slow(value, size):
    for bit in [1 << i for i in range(size.bit_length() - 1)][2:]:
        value = value + send(value, flip(size, bit))
    return value


def sum_fast(value, size):
    for bit in (1, 2):
        value = value + send(value, flip(size, bit))
    return value + send(value, [(0, 1), (1, 0)], "tensor")


def on_device(
    size,
    tokens,
    cotangent,
    picture_ids,
    positions,
    valid,
    norm1_gain,
    norm1_bias,
    qkv_weight,
    qkv_bias,
    proj_weight,
    proj_bias,
    norm2_gain,
    norm2_bias,
    fc1_weight,
    fc1_bias,
    fc2_weight,
    fc2_bias,
):
    me = lax.axis_index("tensor")
    length = picture_ids.shape[0]
    half, model = tokens.shape
    rows = qkv_weight.shape[0]
    width = qkv_weight.shape[2]
    units = fc1_weight.shape[1]
    swap = [(0, 1), (1, 0)]
    cross = lambda value: send(value, swap, "tensor")

    gain_one, shift_one = norm1_gain.astype(f32), norm1_bias.astype(f32)
    gain_two, shift_two = norm2_gain.astype(f32), norm2_bias.astype(f32)
    qkv_shift = lax.dynamic_slice_in_dim(qkv_bias.astype(f32), me * width, width, 1).reshape(1, -1)
    fc1_shift = lax.dynamic_slice_in_dim(fc1_bias.astype(f32), me * units, units, 0).reshape(1, -1)

    where = jnp.stack([me, lax.axis_index("dp")]).astype(jnp.int32)
    inputs = tokens.astype(f32)
    unit_one, inverse_one = norm_parts(inputs)
    a_own = (unit_one * gain_one + shift_one).astype(bf16)
    a_other = cross(a_own)
    tables = rope_tables(positions, width)
    mq, mk = mask_lanes(picture_ids, valid, width // 128 - 1)

    qkv_own = gather_slow(qkv_weight.reshape(rows, 3 * width), size)
    joined = jnp.concatenate([proj_weight.T, fc1_weight], axis=1)
    cosine, down, up = tables
    qkv_own, joined, a_other, cosine, down = tie(qkv_own, joined, a_other, cosine, down)
    qkv_near = gather_near(qkv_own, size)
    own = gather_slow(joined, size)
    qkv_near, up, mq, mk = tie(qkv_near, up, mq, mk)
    qkv_far = gather_far(qkv_near, size)
    qkv_far, own = tie(qkv_far, own)
    tables = (cosine, down, up)
    near = gather_near(own, size)
    (qkv_full,) = place(qkv_own, qkv_near, qkv_far, size, [3 * width])
    q, k, v = qkv_rotate(where, a_own, a_other, qkv_full, qkv_shift, tables)
    pairs = mq.shape[0]
    mixed, lse_low = attend(mq, mk, q, k, v, 0, pairs // 2)
    near, mixed, fc2_shard = tie(near, mixed, fc2_weight.T)
    far = gather_far(near, size)
    fc2_turned = lax.all_gather(fc2_shard, "dp", axis=0, tiled=True)
    mixed, lse_high = attend(mq, mk, q, k, v, pairs // 2, pairs - pairs // 2, (mixed,))
    far, mixed = tie(far, mixed)
    proj_turned, fc1_full = place(own, near, far, size, [width, units])

    away = cross(product_for_other(where, mixed, proj_turned, half))
    middle, c_own = closing(
        where, mixed, proj_turned, [away, tokens], [proj_bias.astype(f32), gain_two, shift_two],
        finish_attention, [f32, bf16], 0, "middle",
    )
    grad_other = cross(cotangent)
    c_other = cross(c_own)
    hidden_own, slope_own = hidden_slope(c_own, fc1_full, fc1_shift)
    hidden_other, slope_other = hidden_slope(c_other, fc1_full, fc1_shift)

    fc2_stacks = weight_grad(where, [cotangent, grad_other], [hidden_own, hidden_other], size)
    fc2_turned, fc2_stacks = tie(fc2_turned, fc2_stacks)
    fc2_got = scatter_far(fc2_stacks, size)
    pre_other, bias_other = pre_grad(grad_other, fc2_turned, slope_other)
    part = product_for_other(where, pre_other, fc1_full, half)
    pre_own, bias_own = pre_grad(cotangent, fc2_turned, slope_own)
    fc2_got, pre_own, pre_other, part = tie(fc2_got, pre_own, pre_other, part)
    fc2_more = scatter_near(fc2_stacks, fc2_got, size)
    away = cross(part)
    fc1_stacks = weight_grad(where, [c_own, c_other], [pre_own, pre_other], size)
    fc2_more, fc1_stacks, pre_own, away, hidden_other = tie(
        fc2_more, fc1_stacks, pre_own, away, hidden_other
    )
    fc1_got = scatter_far(fc1_stacks, size)
    out_part = product_for_other(where, hidden_other, fc2_turned, half)
    (middle_grad, g_own, gain_two_grad, shift_two_grad, proj_shift_grad, fc2_shift_grad) = closing(
        where, pre_own, fc1_full, [away, middle, cotangent], [gain_two],
        finish_middle, [f32, bf16], 4, "middle_grad",
    )
    (output,) = closing(
        where, hidden_own, fc2_turned, [cross(out_part), middle], [fc2_bias.astype(f32)],
        finish_output, [f32], 0, "output",
    )
    fc1_got, g_own, output = tie(fc1_got, g_own, output)
    fc1_more = scatter_near(fc1_stacks, fc1_got, size)
    g_other = cross(g_own)
    mixed_grad = mixed_grad_rows(where, g_own, g_other, proj_turned)
    proj_grad = weight_grad(where, [g_own, g_other], [mixed])
    lse = jnp.concatenate([lse_low, lse_high], axis=0)
    fc1_more, mixed_grad, proj_grad = tie(fc1_more, mixed_grad, proj_grad)
    groups = [(fc2_stacks, fc2_got, fc2_more), (fc1_stacks, fc1_got, fc1_more)]
    kept, got = scatter_slow(groups, size)
    proj_shard = lax.psum_scatter(proj_grad, "dp", scatter_dimension=0, tiled=True)
    kept, mixed_grad = tie(kept, mixed_grad)
    qkv_grad = attend_back(mq, mk, q, k, v, mixed, mixed_grad, lse, tables)
    got, proj_shard, qkv_grad = tie(got, proj_shard, qkv_grad)
    qkv_stacks = weight_grad(where, [a_own, a_other], [qkv_grad], size)
    qkv_stacks, qkv_grad = tie(qkv_stacks, qkv_grad)
    qkv_got = scatter_far(qkv_stacks, size)
    part = product_for_other(where, qkv_grad, qkv_full, half)
    qkv_shift_grad = jnp.sum(qkv_grad.astype(f32), axis=0)
    input_grad, gain_one_grad, shift_one_grad = closing(
        where, qkv_grad, qkv_full, [cross(part), tokens, middle_grad], [gain_one],
        finish_input, [f32], 2, "input_grad",
    )
    fc1_shift_grad = jnp.sum(bias_own, axis=0) + jnp.sum(bias_other, axis=0)
    fc1_place = lax.dynamic_update_slice_in_dim(
        jnp.zeros((2 * units,), f32), fc1_shift_grad, me * units, 0
    )
    qkv_place = lax.dynamic_update_slice_in_dim(
        jnp.zeros((3, 2 * width), f32), qkv_shift_grad.reshape(3, width), me * width, 1
    )
    sums = [
        gain_one_grad, shift_one_grad, qkv_place.reshape(-1), proj_shift_grad,
        gain_two_grad, shift_two_grad, fc1_place, fc2_shift_grad,
    ]
    totals = sum_slow(jnp.concatenate(sums).reshape(-1, 128), size)
    qkv_got, input_grad, totals = tie(qkv_got, input_grad, totals)
    more = scatter_near(qkv_stacks, qkv_got, size)
    more, kept, got, totals = tie(more, kept, got, totals)
    qkv_kept, qkv_got = scatter_slow([(qkv_stacks, qkv_got, more)], size)
    both_shards = scatter_last(kept, got)
    fc2_shard, fc1_shard = both_shards[:, :units], both_shards[:, units:]
    totals = sum_fast(totals, size).reshape(-1)
    qkv_got, totals, fc2_shard, fc1_shard = tie(qkv_got, totals, fc2_shard, fc1_shard)
    qkv_shard = scatter_last(qkv_kept, qkv_got)
    small = []
    for part in sums:
        small.append(totals[: part.shape[0]])
        totals = totals[part.shape[0] :]
    return (
        output,
        input_grad,
        small[0],
        small[1],
        qkv_shard.reshape(rows, 3, width),
        small[2].reshape(3, 2 * width),
        proj_shard.astype(f32).T,
        small[3],
        small[4],
        small[5],
        fc1_shard,
        small[6],
        fc2_shard.astype(f32).T,
        small[7],
    )


def norm_forward(values, gain, shift):
    center = values - jnp.mean(values, axis=-1, keepdims=True)
    inverse = lax.rsqrt(jnp.mean(center * center, axis=-1, keepdims=True) + EPS)
    unit = center * inverse
    return (unit * gain + shift, unit, inverse)


def on_any(
    tokens,
    cotangent,
    picture_ids,
    positions,
    valid,
    norm1_gain,
    norm1_bias,
    qkv_weight,
    qkv_bias,
    proj_weight,
    proj_bias,
    norm2_gain,
    norm2_bias,
    fc1_weight,
    fc1_bias,
    fc2_weight,
    fc2_bias,
):
    tensor_index = lax.axis_index("tensor")
    model_width = tokens.shape[1]
    local_width = qkv_weight.shape[2]
    local_hidden = fc1_weight.shape[1]
    local_heads = local_width // HEAD_DIM
    gain_one = norm1_gain.astype(jnp.float32)
    shift_one = norm1_bias.astype(jnp.float32)
    gain_two = norm2_gain.astype(jnp.float32)
    shift_two = norm2_bias.astype(jnp.float32)
    qkv_shift = lax.dynamic_slice_in_dim(
        qkv_bias.astype(jnp.float32), tensor_index * local_width, local_width, 1
    ).reshape(3 * local_width)
    fc1_shift = lax.dynamic_slice_in_dim(
        fc1_bias.astype(jnp.float32), tensor_index * local_hidden, local_hidden, 0
    )
    qkv_full, proj_full, fc1_full, fc2_full = (
        lax.all_gather(qkv_weight, "dp", axis=0, tiled=True),
        lax.all_gather(proj_weight, "dp", axis=1, tiled=True),
        lax.all_gather(fc1_weight, "dp", axis=0, tiled=True),
        lax.all_gather(fc2_weight, "dp", axis=1, tiled=True),
    )
    qkv_matrix = qkv_full.reshape(model_width, 3 * local_width)
    inputs = tokens.astype(jnp.float32)
    normed_one, unit_one, inverse_one = norm_forward(inputs, gain_one, shift_one)
    attn_in = lax.all_gather(normed_one.astype(jnp.bfloat16), "tensor", axis=0, tiled=True)
    total_rows = attn_in.shape[0]
    qkv_raw = jnp.dot(attn_in, qkv_matrix, preferred_element_type=jnp.float32) + qkv_shift
    pairs = -(-local_heads // 2)
    padded = 128 * (pairs + 1)
    fill = lambda value: jnp.pad(value, ((0, 0), (0, padded - local_width)))
    tables = [fill(table) for table in rope_tables(positions, local_width)]
    mq, mk = mask_lanes(picture_ids, valid, pairs)

    def rotate(part):
        turned = jnp.roll(part, -HEAD_DIM // 2, 1) * tables[1]
        return part * tables[0] + turned + jnp.roll(part, HEAD_DIM // 2, 1) * tables[2]

    split = [fill(part) for part in jnp.split(qkv_raw, 3, axis=1)]
    queries = (rotate(split[0]) * (HEAD_DIM**-0.5 * LOG2E)).astype(jnp.bfloat16)
    keys = rotate(split[1]).astype(jnp.bfloat16)
    values = split[2].astype(jnp.bfloat16)
    mixed_row, logsum_row = attend(mq, mk, queries, keys, values)
    attn_mixed = mixed_row[:, :local_width]
    piece = attn_mixed
    attn_out = lax.psum_scatter(
        jnp.dot(piece, proj_full, preferred_element_type=jnp.float32).astype(jnp.bfloat16),
        "tensor",
        scatter_dimension=0,
        tiled=True,
    ).astype(jnp.float32) + proj_bias.astype(jnp.float32)
    middle = inputs + attn_out
    normed_two, unit_two, inverse_two = norm_forward(middle, gain_two, shift_two)
    mlp_in = lax.all_gather(normed_two.astype(jnp.bfloat16), "tensor", axis=0, tiled=True)
    hidden_pre = jnp.dot(mlp_in, fc1_full, preferred_element_type=jnp.float32) + fc1_shift
    sigmoid_gate = jax.nn.sigmoid(1.702 * hidden_pre)
    hidden = (hidden_pre * sigmoid_gate).astype(jnp.bfloat16)
    piece = hidden
    mlp_out = lax.psum_scatter(
        jnp.dot(piece, fc2_full, preferred_element_type=jnp.float32).astype(jnp.bfloat16),
        "tensor",
        scatter_dimension=0,
        tiled=True,
    ).astype(jnp.float32) + fc2_bias.astype(jnp.float32)
    output = middle + mlp_out
    qkv_back, proj_back, fc1_back, fc2_back = (
        lax.all_gather(qkv_weight, "dp", axis=0, tiled=True),
        lax.all_gather(proj_weight, "dp", axis=1, tiled=True),
        lax.all_gather(fc1_weight, "dp", axis=0, tiled=True),
        lax.all_gather(fc2_weight, "dp", axis=1, tiled=True),
    )
    qkv_back = qkv_back.reshape(model_width, 3 * local_width)
    out_grad = cotangent.astype(jnp.float32)
    fc2_shift_grad = jnp.sum(out_grad, axis=0)
    out_grad_full = lax.all_gather(cotangent, "tensor", axis=0, tiled=True)
    fc2_grad = jnp.dot(hidden.T, out_grad_full, preferred_element_type=jnp.float32)
    hidden_grad = jnp.dot(out_grad_full, fc2_back.T, preferred_element_type=jnp.float32)
    slope = sigmoid_gate + 1.702 * hidden_pre * sigmoid_gate * (1.0 - sigmoid_gate)
    pre_grad = (hidden_grad * slope).astype(jnp.bfloat16)
    fc1_shift_grad = jnp.sum(pre_grad.astype(jnp.float32), axis=0)
    fc1_grad = jnp.dot(mlp_in.T, pre_grad, preferred_element_type=jnp.float32)
    piece = pre_grad
    normed_two_grad = lax.psum_scatter(
        jnp.dot(piece, fc1_back.T, preferred_element_type=jnp.float32).astype(jnp.bfloat16),
        "tensor",
        scatter_dimension=0,
        tiled=True,
    ).astype(jnp.float32)
    middle_part, gain_two_grad, shift_two_grad = norm_backward(
        normed_two_grad, unit_two, inverse_two, gain_two
    )
    middle_grad = out_grad + middle_part
    attn_grad_low = middle_grad.astype(jnp.bfloat16)
    proj_shift_grad = jnp.sum(attn_grad_low.astype(jnp.float32), axis=0)
    attn_grad_full = lax.all_gather(attn_grad_low, "tensor", axis=0, tiled=True)
    proj_grad = jnp.dot(attn_mixed.T, attn_grad_full, preferred_element_type=jnp.float32)
    mixed_grad = jnp.dot(attn_grad_full, proj_back.T, preferred_element_type=jnp.float32).astype(
        jnp.bfloat16
    )
    qkv_grad = attend_back(
        mq, mk, queries, keys, values, mixed_row, fill(mixed_grad), logsum_row, tables
    )
    qkv_grad = jnp.concatenate(
        [qkv_grad[:, at : at + local_width] for at in (0, padded, 2 * padded)], axis=1
    )
    qkv_shift_grad = jnp.sum(qkv_grad.astype(jnp.float32), axis=0)
    qkv_grad_weight = jnp.dot(attn_in.T, qkv_grad, preferred_element_type=jnp.float32)
    qkv_grad_weight = qkv_grad_weight.reshape(model_width, 3, local_width)
    piece = qkv_grad
    normed_one_grad = lax.psum_scatter(
        jnp.dot(piece, qkv_back.T, preferred_element_type=jnp.float32).astype(jnp.bfloat16),
        "tensor",
        scatter_dimension=0,
        tiled=True,
    ).astype(jnp.float32)
    input_part, gain_one_grad, shift_one_grad = norm_backward(
        normed_one_grad, unit_one, inverse_one, gain_one
    )
    input_grad = middle_grad + input_part
    qkv_grad_shard, proj_grad_shard, fc1_grad_shard, fc2_grad_shard = (
        lax.psum_scatter(
            qkv_grad_weight.astype(jnp.bfloat16), "dp", scatter_dimension=0, tiled=True
        ).astype(jnp.float32),
        lax.psum_scatter(
            proj_grad.astype(jnp.bfloat16), "dp", scatter_dimension=1, tiled=True
        ).astype(jnp.float32),
        lax.psum_scatter(
            fc1_grad.astype(jnp.bfloat16), "dp", scatter_dimension=0, tiled=True
        ).astype(jnp.float32),
        lax.psum_scatter(
            fc2_grad.astype(jnp.bfloat16), "dp", scatter_dimension=1, tiled=True
        ).astype(jnp.float32),
    )
    qkv_shift_full = lax.dynamic_update_slice_in_dim(
        jnp.zeros((3, model_width), jnp.float32),
        qkv_shift_grad.reshape(3, local_width),
        tensor_index * local_width,
        1,
    )
    fc1_shift_full = lax.dynamic_update_slice_in_dim(
        jnp.zeros((fc1_bias.shape[0],), jnp.float32), fc1_shift_grad, tensor_index * local_hidden, 0
    )
    summed = lax.psum(
        (
            gain_one_grad,
            shift_one_grad,
            qkv_shift_full,
            proj_shift_grad,
            gain_two_grad,
            shift_two_grad,
            fc1_shift_full,
            fc2_shift_grad,
        ),
        ("dp", "tensor"),
    )
    return (
        output,
        input_grad,
        summed[0],
        summed[1],
        qkv_grad_shard,
        summed[2],
        proj_grad_shard,
        summed[3],
        summed[4],
        summed[5],
        fc1_grad_shard,
        summed[6],
        fc2_grad_shard,
        summed[7],
    )


def solution(mesh):
    size = mesh.shape["dp"]
    paired = mesh.shape["tensor"] == 2 and size == 16
    return jax.shard_map(
        functools.partial(on_device, size) if paired else on_any,
        mesh=mesh,
        in_specs=(
            P(("dp", "tensor"), None),
            P(("dp", "tensor"), None),
            P("dp"),
            P(None, "dp"),
            P("dp"),
            P(),
            P(),
            P("dp", None, "tensor"),
            P(),
            P("tensor", "dp"),
            P(),
            P(),
            P(),
            P("dp", "tensor"),
            P(),
            P("tensor", "dp"),
            P(),
        ),
        out_specs=(
            P(("dp", "tensor"), None),
            P(("dp", "tensor"), None),
            P(),
            P(),
            P("dp", None, "tensor"),
            P(),
            P("tensor", "dp"),
            P(),
            P(),
            P(),
            P("dp", "tensor"),
            P(),
            P("tensor", "dp"),
            P(),
        ),
        check_vma=False,
    )
```
